256 devices in a mesh: row: 8 (over y, x_lo), col: 32 (over z, x_hi, core).
Axes of the slice: x: 4 (x_hi: 2, x_lo: 2; x = x_hi * 2 + x_lo), y: 4, z: 8, core: 2. Of those that a mesh axis runs over, the one named last changes fastest.
Arguments:
- features: bfloat16 [49152, 256], P(('col', 'row')), may hold values from -6 to 6
- weight: bfloat16 [256, 256], replicated, may hold values from -0.375 to 0.375
- src_degree: int32 [49152], P(('col', 'row')), may hold values from 12 to 744
- dst_degree: int32 [49152], P(('row', 'col')), may hold values from 12 to 744
- cotangent: bfloat16 [49152, 256], P(('row', 'col')), may hold values from -6 to 6
- tile_rows: int32 [49152], P(('row', 'col')), may hold values from 0 to 47
- tile_cols: int32 [49152], P(('row', 'col')), may hold values from 0 to 11
- tile_count: int32 [256], P(('row', 'col')), may hold values from 1 to 192, as said below
- pattern: int32 [49152, 16, 128], P(('row', 'col')), may hold values from 0 to 255
Outputs:
- activations: bfloat16 [49152, 256], P(('row', 'col'))
- grad_features: bfloat16 [49152, 256], P(('col', 'row'))
- grad_weight: float32 [256, 256], replicated
The draws below stay inside these ranges and needn't reach their ends.
Inputs may be any that keep to these rules, and one draw needn't show every extreme that they name: Only the first tile_count[g] slots of group g hold tiles; the coordinates and patterns of its other slots are not part of the adjacency. Some group uses all 192 slots. `tile_rows`: slots of one group may name the same tile position.
All inputs are finite; a program needn't handle non-finite values.
Results may differ from the reference program's by a relative error of at most 0.0058.
Values may be sent and summed in bfloat16 or wider, within the bound.
A program may use at most 128 MiB of HBM per device.

```python
import jax
import jax.numpy as jnp
from jax import lax

FEAT = 256
TILE = 128
SLOTS = 192
DEVICE_COUNT = 256
COL_GROUPS = 32
NODES = 49152
ROW_SPAN = 6144
COL_SPAN = 1536
TROWS = 48
TCOLS = 12
ALL_SLOTS = 49152


def degree_values(key):
    mantissa_key, exponent_key = jax.random.split(key)
    mantissa = jax.random.randint(mantissa_key, (NODES,), 16, 32, dtype=jnp.int32)
    exponent = jax.random.randint(exponent_key, (NODES,), 0, 6, dtype=jnp.int32)
    return (max(1, NODES // 4096) * (jnp.left_shift(mantissa, exponent) // 16)).astype(jnp.int32)


def draw_src_degree(key, part):
    key = jax.random.fold_in(key, 11)
    return degree_values(key)


def draw_dst_degree(key, part):
    key = jax.random.fold_in(key, 13)
    return degree_values(key)


def draw_tile_count(key, part):
    key = jax.random.fold_in(key, 17)
    mantissa_key, exponent_key, busiest_key = jax.random.split(key, 3)
    mantissa = jax.random.randint(mantissa_key, (DEVICE_COUNT,), 8, 17, dtype=jnp.int32)
    exponent = jax.random.randint(exponent_key, (DEVICE_COUNT,), 0, 4, dtype=jnp.int32)
    counts = jnp.maximum(1, SLOTS * mantissa // jnp.left_shift(jnp.int32(16), exponent))
    busiest = jax.random.randint(busiest_key, (), 0, DEVICE_COUNT, dtype=jnp.int32)
    return jnp.where(jnp.arange(DEVICE_COUNT, dtype=jnp.int32) == busiest, SLOTS, counts).astype(jnp.int32)


def three_bytes(key, array_shape):
    word_bits = jax.random.randint(key, array_shape, 0, 2 ** 30, dtype=jnp.int32)
    first_byte = jnp.bitwise_and(word_bits, 255)
    second_byte = jnp.bitwise_and(jnp.right_shift(word_bits, 8), 255)
    third_byte = jnp.bitwise_and(jnp.right_shift(word_bits, 16), 255)
    return jnp.bitwise_and(jnp.bitwise_and(first_byte, second_byte), third_byte)


def draw_pattern(key, part):
    key = jax.random.fold_in(key, 19)
    first_key, second_key, dense_key, source_key = jax.random.split(key, 4)
    array_shape = (ALL_SLOTS, TILE // 8, TILE)
    sparse_bits = jnp.bitwise_and(three_bytes(first_key, array_shape), three_bytes(second_key, array_shape))
    dense_bits = jax.random.randint(dense_key, array_shape, 0, 256, dtype=jnp.int32)
    hub_column = jax.random.randint(source_key, (ALL_SLOTS, 1, TILE), 0, 32, dtype=jnp.int32) == 0
    return jnp.where(hub_column, dense_bits, sparse_bits).astype(jnp.int32)


def place_ends(drawn, key, low, largest):
    longest = drawn.shape.index(max(drawn.shape))
    spots = []
    for shift in (0, 1):
        where = [jax.random.randint(jax.random.fold_in(key, axis), (), 0, length) for axis, length in enumerate(drawn.shape)]
        where[longest] = (where[longest] + shift) % drawn.shape[longest]
        spots.append(tuple(where))
    return drawn.at[spots[0]].set(low).at[spots[1]].set(largest)


def levels(own_key, dims, cuts, least, top_value):
    gain, own = 1.0, jax.random.fold_in(own_key, 6)
    for position, parts in cuts:
        steps = jnp.exp(jax.random.uniform(jax.random.fold_in(own, position), (parts,), jnp.float32, least / len(cuts), top_value / len(cuts)))
        gain = gain * jnp.repeat(steps, dims[position] // parts).reshape([-1 if axis == position else 1 for axis in range(len(dims))])
    return gain


def bell_draw(own_key, extent, scale, reach, shards=(), held_as=jnp.bfloat16):
    gain = levels(own_key, extent, shards, -0.22, 0.18) if shards else 1.0
    array = jax.random.normal(own_key, extent, jnp.float32) * scale * gain
    return jnp.minimum(jnp.maximum(array, -reach), reach).astype(held_as)


def setup_inputs(seed: int = 0) -> dict:
    streams_of = jax.random.split(jax.random.key(seed), 10)
    features = bell_draw(streams_of[0], (NODES, FEAT), 1.0, 6.0, ((0, 256),))
    weight = bell_draw(streams_of[1], (FEAT, FEAT), FEAT ** -0.5, 0.375)
    src_degree = draw_src_degree(jax.random.fold_in(streams_of[9], 71), 0)
    dst_degree = draw_dst_degree(jax.random.fold_in(streams_of[9], 71), 0)
    cotangent = bell_draw(streams_of[4], (NODES, FEAT), 1.0, 6.0, ((0, 256),))
    tile_rows = place_ends(jax.random.randint(streams_of[5], (ALL_SLOTS,), 0, TROWS), jax.random.fold_in(streams_of[5], 1), 0, TROWS - 1).astype(jnp.int32)
    tile_cols = place_ends(jax.random.randint(streams_of[6], (ALL_SLOTS,), 0, TCOLS), jax.random.fold_in(streams_of[6], 1), 0, TCOLS - 1).astype(jnp.int32)
    tile_count = draw_tile_count(jax.random.fold_in(streams_of[9], 71), 0)
    pattern = draw_pattern(jax.random.fold_in(streams_of[9], 71), 0)
    return {"features": features, "weight": weight, "src_degree": src_degree, "dst_degree": dst_degree, "cotangent": cotangent, "tile_rows": tile_rows, "tile_cols": tile_cols, "tile_count": tile_count, "pattern": pattern}


def unpack_block(packed, alive_mask):
    offsets = jnp.arange(8, dtype=jnp.int32)
    spread = jnp.bitwise_and(jnp.right_shift(packed[:, :, None, :], offsets[None, None, :, None]), 1)
    square = spread.reshape(packed.shape[0], packed.shape[1] * 8, packed.shape[2])
    return (square * alive_mask[:, None, None]).astype(jnp.float32)

def elu_value(preact):
    return jnp.where(preact > 0, preact, jnp.expm1(jnp.minimum(preact, 0.0)))

def elu_slope(preact):
    return jnp.where(preact > 0, 1.0, jnp.exp(jnp.minimum(preact, 0.0)))

def reference(features, weight, src_degree, dst_degree, cotangent, tile_rows, tile_cols, tile_count, pattern):
    src_scale = lax.rsqrt(src_degree.astype(jnp.float32))
    dst_scale = lax.rsqrt(dst_degree.astype(jnp.float32))
    hidden = jnp.dot(features, weight, preferred_element_type=jnp.float32)
    scaled = (src_scale[:, None] * hidden).astype(jnp.bfloat16)
    slot_all = jnp.arange(ALL_SLOTS, dtype=jnp.int32)
    group_index = slot_all // SLOTS
    alive_slots = (slot_all % SLOTS < tile_count[group_index]).astype(jnp.int32)
    row_start = group_index // COL_GROUPS * ROW_SPAN + tile_rows * TILE
    col_start = group_index % COL_GROUPS * COL_SPAN + tile_cols * TILE
    within = jnp.arange(TILE, dtype=jnp.int32)
    blocks = (row_start.reshape(DEVICE_COUNT, SLOTS), col_start.reshape(DEVICE_COUNT, SLOTS), pattern.reshape(DEVICE_COUNT, SLOTS, TILE // 8, TILE), alive_slots.reshape(DEVICE_COUNT, SLOTS))

    def forward_step(accumulator, slot_block):
        row_first, col_first, packed, alive_mask = slot_block
        square = unpack_block(packed, alive_mask)
        pulled = scaled[col_first[:, None] + within[None, :]].astype(jnp.float32)
        product = jnp.einsum('brc,bcf->brf', square, pulled)
        return (accumulator.at[row_first[:, None] + within[None, :]].add(product), None)
    row_sums = lax.scan(forward_step, jnp.zeros((NODES, FEAT), jnp.float32), blocks)[0]
    preact = dst_scale[:, None] * row_sums
    activations = elu_value(preact).astype(jnp.bfloat16)
    grad_rows = (dst_scale[:, None] * (cotangent.astype(jnp.float32) * elu_slope(preact))).astype(jnp.bfloat16)

    def backward_step(accumulator, slot_block):
        row_first, col_first, packed, alive_mask = slot_block
        square = unpack_block(packed, alive_mask)
        pulled = grad_rows[row_first[:, None] + within[None, :]].astype(jnp.float32)
        product = jnp.einsum('brc,brf->bcf', square, pulled)
        return (accumulator.at[col_first[:, None] + within[None, :]].add(product), None)
    col_sums = lax.scan(backward_step, jnp.zeros((NODES, FEAT), jnp.float32), blocks)[0]
    grad_hidden = (src_scale[:, None] * col_sums).astype(jnp.bfloat16)
    grad_features = jnp.dot(grad_hidden, weight.T, preferred_element_type=jnp.float32).astype(jnp.bfloat16)
    weight_sum = jnp.dot(features.T, grad_hidden, preferred_element_type=jnp.float32)
    root_mean = jnp.sqrt(jnp.mean(weight_sum * weight_sum))
    grad_weight = weight_sum * jnp.minimum(1.0, 1.0 / (root_mean + 1e-06))
    return (activations, grad_features, grad_weight)
```

```python
import functools

import jax
import jax.numpy as jnp
from jax import lax
from jax.experimental import pallas as pl
from jax.experimental.pallas import tpu as pltpu
from jax.sharding import PartitionSpec as P

MESH = pl.DeviceIdType.MESH
F32 = jnp.float32
BF16 = jnp.bfloat16

FEAT = 256
HALF = 128
TILE = 128
SLOTS = 192
OWN = 192
ROWS = 8
RING = 8
TROWS = 48
TCOLS = 12
PLACES = TROWS * TCOLS
CHUNK = 4 * OWN
ROW_SPAN = RING * CHUNK
COL_SPAN = ROWS * OWN
PIECE = FEAT // ROWS
QUARTER = PIECE // 4


def place_table(tile_rows, tile_cols, tile_count):
    slots = jnp.arange(SLOTS, dtype=jnp.int32)
    place = jnp.where(slots < tile_count[0], tile_rows * TCOLS + tile_cols, -1)
    asked = jnp.concatenate([jnp.arange(PLACES, dtype=jnp.int32), place])
    before = jnp.concatenate([jnp.full((PLACES,), SLOTS, jnp.int32), slots])
    named = (place[None, :] == asked[:, None]) & (slots[None, :] < before[:, None])
    named = named & (place[None, :] >= 0)
    last = jnp.max(jnp.where(named, slots[None, :], -1), axis=1)
    return jnp.where(last < 0, SLOTS, last)


def remote(src, dst, send_sem, recv_sem, device):
    return pltpu.make_async_remote_copy(
        src_ref=src,
        dst_ref=dst,
        send_sem=send_sem,
        recv_sem=recv_sem,
        device_id=device,
        device_id_type=MESH,
    )


def rows_at(start, size):
    return pl.ds(pl.multiple_of(start, 8 if size < 16 else 32), size)


def kernel(
    table,
    feat,
    weight,
    src_deg,
    dst_deg,
    cot,
    pattern,
    act_out,
    gf_out,
    gw_out,
    deg_buf,
    s_all,
    tiles,
    adj,
    part,
    core_out,
    core_in,
    first_out,
    first_in,
    ring_out,
    ring_in,
    xhi_out,
    xhi_in,
    grads,
    acc,
    cols_f,
    cols_b,
    cols_in,
    w_part,
    w_rows,
    w_quart,
    w_ring,
    w_full,
    gat_s,
    gat_r,
    core_s,
    core_r,
    ring_s,
    ring_r,
    xhi_s,
    xhi_r,
    agr_s,
    agr_r,
    agc_s,
    agc_r,
    agx_s,
    agx_r,
    col_s,
    col_r,
    w1_s,
    w1_r,
    w2_s,
    w2_r,
    w3_s,
    w3_r,
    w4_s,
    w4_r,
    w5_s,
    w5_r,
):
    r = lax.axis_index("row")
    c = lax.axis_index("col")
    z = c // 4
    quad = c % 4
    xhi = quad // 2
    core = quad % 2
    other_core = 1 - core
    other_xhi = 1 - xhi

    def row_dev(i):
        return {"row": (r + i) % ROWS}

    def quad_dev(i):
        return {"col": z * 4 + (quad + i) % 4}

    def z_dev(i):
        return {"col": ((z + i) % RING) * 4 + quad}

    core_dev = {"col": z * 4 + xhi * 2 + other_core}
    xhi_dev = {"col": z * 4 + other_xhi * 2 + core}
    ring_dev = [z_dev(1), z_dev(RING - 1)]

    barrier = pltpu.get_barrier_semaphore()

    def greet(device):
        pl.semaphore_signal(barrier, inc=1, device_id=device, device_id_type=MESH)

    def greet_rows(i, _):
        greet(row_dev(i))
        greet(z_dev(i))
        return 0

    def greet_quad(i, _):
        greet(quad_dev(i))
        return 0

    lax.fori_loop(1, ROWS, greet_rows, 0)
    lax.fori_loop(1, 4, greet_quad, 0)
    pl.semaphore_wait(barrier, 2 * (ROWS - 1) + 3)

    def column(deg):
        deg_buf[...] = jnp.ones_like(deg_buf)
        scale = lax.rsqrt(deg[...].astype(F32))
        deg_buf[:, 0:OWN] = jnp.broadcast_to(scale, (HALF, OWN))
        turned = deg_buf[...].T[0:OWN, :]
        return jnp.concatenate([turned, turned], axis=1)

    src_scale = column(src_deg)
    own_rows = rows_at(r * OWN, OWN)
    s_all[own_rows, :] = (feat[...].astype(F32) * src_scale).astype(BF16)

    def gather_copy(i, sender):
        span = rows_at(sender * OWN, OWN)
        return remote(s_all.at[span], s_all.at[span], gat_s.at[i - 1], gat_r.at[i - 1], row_dev(i))

    def gather_start(i, _):
        gather_copy(i, r).start()
        return 0

    lax.fori_loop(1, ROWS, gather_start, 0)

    tiles[SLOTS] = jnp.zeros((TILE, TILE), BF16)
    bit = lax.broadcasted_iota(jnp.int32, (TILE // 8, 8, TILE), 1)

    def unpack(k, _):
        words = jnp.broadcast_to(pattern[k][:, None, :], (TILE // 8, 8, TILE))
        bits = jnp.bitwise_and(jnp.right_shift(words, bit), 1).reshape(TILE, TILE)
        tiles[k] = bits.astype(F32).astype(BF16) + tiles[table[PLACES + k]]
        return 0

    lax.fori_loop(0, SLOTS, unpack, 0)

    def assemble(t, _):
        for j in range(TCOLS):
            adj[rows_at(t * TILE, TILE), j * TILE : (j + 1) * TILE] = tiles[table[t * TCOLS + j]]
        return 0

    lax.fori_loop(0, TROWS, assemble, 0)

    def gather_wait(i, _):
        gather_copy(i, (r + ROWS - i) % ROWS).wait_recv()
        return 0

    lax.fori_loop(1, ROWS, gather_wait, 0)

    def core_copy(i):
        return remote(core_out.at[i], core_in.at[i], core_s.at[i], core_r.at[i], core_dev)

    def stream(q):
        return other_xhi if q == 0 else xhi

    def chip_sum(i, q):
        xh = stream(q)
        mine = part[i, rows_at((2 * xh + core) * OWN, OWN), :]
        return mine + core_in[i, xh].astype(F32)

    def first_copy(way, q):
        return remote(
            first_out.at[way, q],
            first_in.at[way, q],
            ring_s.at[way, 0, q],
            ring_r.at[way, 0, q],
            ring_dev[way],
        )

    def ring_copy(way, step, q):
        return remote(
            ring_out.at[way, step - 1, q],
            ring_in.at[way, step - 1, q],
            ring_s.at[way, step, q],
            ring_r.at[way, step, q],
            ring_dev[way],
        )

    def ring_step(step):
        if step == 0:
            core_copy(0).wait_recv()
            for q in range(2):
                total = chip_sum(0, q)
                for way in range(2):
                    first_out[way, q] = total[:, way * HALF : (way + 1) * HALF].astype(BF16)
                    first_copy(way, q).start()
            return
        core_copy(2 * step - 1).wait_recv()
        core_copy(2 * step).wait_recv()
        for q in range(2):
            for way in range(2):
                total = chip_sum(2 * step - 1 + way, q)
                if step == 1:
                    first_copy(way, q).wait_recv()
                    arrived = first_in[way, q].astype(F32)
                    for half in range(2):
                        lanes = slice(half * HALF, (half + 1) * HALF)
                        block = total[:, lanes]
                        if half == way:
                            block = block + arrived
                        ring_out[way, 0, q, :, lanes] = block.astype(BF16)
                else:
                    ring_copy(way, step - 1, q).wait_recv()
                    total = total + ring_in[way, step - 2, q].astype(F32)
                    ring_out[way, step - 1, q] = total.astype(BF16)
                ring_copy(way, step, q).start()

    def forward_chunk(i, _):
        back = 4 - (i + 1) // 2
        there = (z + jnp.where(i % 2 == 1, back, RING - back)) % RING
        part[i] = jnp.dot(
            adj[rows_at(there * CHUNK, CHUNK), :], s_all[...], preferred_element_type=F32
        )
        for xh in range(2):
            theirs = part[i, rows_at((2 * xh + other_core) * OWN, OWN), :]
            core_out[i, xh] = theirs.astype(BF16)
        core_copy(i).start()
        for at, step in ((1, 0), (3, 1), (6, 2), (7, 3)):
            pl.when(i == at)(functools.partial(ring_step, step))
        return 0

    lax.fori_loop(0, RING, forward_chunk, 0)

    core_copy(7).wait_recv()

    def home_sum(q):
        total = chip_sum(7, q)
        for way in range(2):
            ring_copy(way, 3, q).wait_recv()
            total = total + ring_in[way, 2, q].astype(F32)
        return total

    xhi_out[...] = home_sum(0).astype(BF16)
    xhi_copy = remote(xhi_out, xhi_in, xhi_s, xhi_r, xhi_dev)
    xhi_copy.start()
    home = home_sum(1)
    xhi_copy.wait_recv()
    sums = home + xhi_in[...].astype(F32)

    dst_scale = column(dst_deg)
    high = sums.astype(BF16)
    low = (sums - high.astype(F32)).astype(BF16)
    mixed = jnp.dot(high, weight[...], preferred_element_type=F32)
    mixed = mixed + jnp.dot(low, weight[...], preferred_element_type=F32)
    preact = dst_scale * mixed
    decay = jnp.exp(jnp.minimum(preact, 0.0))
    act_out[...] = jnp.where(preact > 0, preact, decay - 1.0).astype(BF16)
    slope = jnp.where(preact > 0, 1.0, decay)
    grad_own = (dst_scale * (cot[...].astype(F32) * slope)).astype(BF16)

    def block_rows(chip, xh, cr):
        return rows_at(chip * CHUNK + (2 * xh + cr) * OWN, OWN)

    def same(rows, lanes, send_sem, recv_sem, device):
        ref = grads.at[rows] if lanes is None else grads.at[rows, lanes]
        return remote(ref, ref, send_sem, recv_sem, device)

    sides = (xhi, other_xhi)
    grads[block_rows(z, xhi, core), :] = grad_own

    def origin(way, distance):
        return (z + (RING - distance if way == 0 else distance)) % RING

    def lanes_of(way, distance):
        return pl.ds(way * HALF, HALF) if distance == 4 else None

    def around(way, distance, st, chip):
        return same(
            block_rows(chip, sides[st], core),
            lanes_of(way, distance),
            agr_s.at[way, distance - 1, st],
            agr_r.at[way, distance - 1, st],
            ring_dev[way],
        )

    def across(way, distance, st, cr):
        if distance == 0:
            sems = agc_s.at[0, 0, st], agc_r.at[0, 0, st]
            return same(block_rows(z, sides[st], cr), None, *sems, core_dev)
        sems = agc_s.at[way, distance, st], agc_r.at[way, distance, st]
        rows = block_rows(origin(way, distance), sides[st], cr)
        return same(rows, lanes_of(way, distance), *sems, core_dev)

    def xhi_gather(xh):
        return same(block_rows(z, xh, core), None, agx_s, agx_r, xhi_dev)

    xhi_gather(xhi).start()
    for way in range(2):
        around(way, 1, 0, z).start()
    across(0, 0, 0, core).start()

    turn = (((0,), (0,)), ((), ()))
    w_part[...] = lax.dot_general(
        high, grad_own, turn, preferred_element_type=F32
    ) + lax.dot_general(low, grad_own, turn, preferred_element_type=F32)

    def w1_copy(i):
        mine = w_part.at[rows_at(((r + i) % ROWS) * PIECE, PIECE)]
        return remote(mine, w_rows.at[i - 1], w1_s.at[i - 1], w1_r.at[i - 1], row_dev(i))

    def w2_copy(i):
        start = r * PIECE + ((quad + i) % 4) * QUARTER
        mine = w_part.at[rows_at(start, QUARTER)]
        return remote(mine, w_quart.at[i - 1], w2_s.at[i - 1], w2_r.at[i - 1], quad_dev(i))

    def w3_copy(i, sender):
        return remote(
            w_ring.at[sender], w_ring.at[sender], w3_s.at[i - 1], w3_r.at[i - 1], z_dev(i)
        )

    def w4_copy(i, sender):
        ref = w_full.at[rows_at(r * PIECE + sender * QUARTER, QUARTER)]
        return remote(ref, ref, w4_s.at[i - 1], w4_r.at[i - 1], quad_dev(i))

    def w5_copy(i, sender):
        ref = w_full.at[rows_at(sender * PIECE, PIECE)]
        return remote(ref, ref, w5_s.at[i - 1], w5_r.at[i - 1], row_dev(i))

    def each(count, action):
        def body(i, _):
            action(i)
            return 0

        lax.fori_loop(1, count, body, 0)

    def w_stage1():
        each(ROWS, lambda i: w1_copy(i).start())

    def w_stage2():
        each(ROWS, lambda i: w1_copy(i).wait_recv())
        piece = rows_at(r * PIECE, PIECE)
        total = w_part[piece, :]
        for i in range(ROWS - 1):
            total = total + w_rows[i]
        w_part[piece, :] = total
        each(4, lambda i: w2_copy(i).start())

    def w_stage3():
        each(4, lambda i: w2_copy(i).wait_recv())
        total = w_part[rows_at(r * PIECE + quad * QUARTER, QUARTER), :]
        for i in range(3):
            total = total + w_quart[i]
        w_ring[z] = total
        each(RING, lambda i: w3_copy(i, z).start())

    def w_stage4():
        each(RING, lambda i: w3_copy(i, (z + RING - i) % RING).wait_recv())
        total = w_ring[0]
        for i in range(1, RING):
            total = total + w_ring[i]
        w_full[rows_at(r * PIECE + quad * QUARTER, QUARTER), :] = total
        each(4, lambda i: w4_copy(i, quad).start())

    def w_stage5():
        each(4, lambda i: w4_copy(i, (quad + 4 - i) % 4).wait_recv())
        each(ROWS, lambda i: w5_copy(i, r).start())

    w_stage1()

    xhi_gather(other_xhi).wait_recv()
    for way in range(2):
        around(way, 1, 1, z).start()
    across(0, 0, 1, core).start()

    acc[...] = jnp.zeros_like(acc)

    def arrive(distance):
        for st in range(2):
            for way in range(2):
                chip = origin(way, distance)
                around(way, distance, st, chip).wait_recv()
                if distance < 3:
                    around(way, distance + 1, st, chip).start()
                elif distance == 3:
                    around(way, 4, st, chip).start()
                across(way, distance, st, core).start()

    def cross_wait(distance, ways):
        for st in range(2):
            for way in ways:
                across(way, distance, st, other_core).wait_recv()

    def backward_chunk(i, _):
        pl.when(i == 0)(functools.partial(cross_wait, 0, (0,)))
        for distance in range(1, 4):
            for way in range(2):
                at = 2 * distance - 1 + way
                pl.when(i == at)(functools.partial(cross_wait, distance, (way,)))
        pl.when(i == 7)(functools.partial(cross_wait, 4, (0, 1)))
        away = (i + 1) // 2
        there = (z + jnp.where(i % 2 == 1, RING - away, away)) % RING
        span = rows_at(there * CHUNK, CHUNK)
        turned = grads[span, :].T

        def columns(j, _):
            lanes = pl.ds(pl.multiple_of(j * FEAT, FEAT), FEAT)
            acc[:, lanes] += jnp.dot(turned, adj[span, lanes], preferred_element_type=F32)
            return 0

        lax.fori_loop(0, COL_SPAN // FEAT, columns, 0)
        for distance in range(1, 5):
            pl.when(i == 2 * (distance - 1))(functools.partial(arrive, distance))
        pl.when(i == 1)(w_stage2)
        pl.when(i == 3)(w_stage3)
        pl.when(i == 5)(w_stage4)
        pl.when(i == 6)(w_stage5)
        return 0

    lax.fori_loop(0, RING, backward_chunk, 0)

    def turn_back(t, _):
        lanes = pl.ds(pl.multiple_of(t * TILE, TILE), TILE)
        block = acc[:, lanes].T
        span = rows_at(t * TILE, TILE)
        cols_f[span, :] = block
        cols_b[span, :] = block.astype(BF16)
        return 0

    lax.fori_loop(0, TCOLS, turn_back, 0)

    def col_copy(i):
        mine = cols_b.at[rows_at(((r + i) % ROWS) * OWN, OWN)]
        return remote(mine, cols_in.at[i - 1], col_s.at[i - 1], col_r.at[i - 1], row_dev(i))

    each(ROWS, lambda i: col_copy(i).start())

    each(ROWS, lambda i: w5_copy(i, (r + ROWS - i) % ROWS).wait_recv())
    full = w_full[...]
    root = jnp.sqrt(jnp.sum(full * full) * (1.0 / (FEAT * FEAT)))
    gw_out[...] = full * jnp.minimum(1.0, 1.0 / (root + 1e-6))

    src_again = column(src_deg)
    each(ROWS, lambda i: col_copy(i).wait_recv())
    total = cols_f[own_rows, :]
    for i in range(ROWS - 1):
        total = total + cols_in[i].astype(F32)
    hidden = (src_again * total).astype(BF16)
    gf_out[...] = lax.dot_general(
        hidden, weight[...], (((1,), (1,)), ((), ())), preferred_element_type=F32
    ).astype(BF16)

    each(ROWS, lambda i: gather_copy(i, r).wait_send())
    each(ROWS, lambda i: col_copy(i).wait_send())
    each(ROWS, lambda i: w1_copy(i).wait_send())
    each(4, lambda i: w2_copy(i).wait_send())
    each(RING, lambda i: w3_copy(i, z).wait_send())
    each(4, lambda i: w4_copy(i, quad).wait_send())
    each(ROWS, lambda i: w5_copy(i, r).wait_send())
    for i in range(RING):
        core_copy(i).wait_send()
    xhi_copy.wait_send()
    xhi_gather(xhi).wait_send()
    for st in range(2):
        across(0, 0, st, core).wait_send()
        for way in range(2):
            first_copy(way, st).wait_send()
            for step in range(1, 4):
                ring_copy(way, step, st).wait_send()
            for distance in range(1, 5):
                around(way, distance, st, origin(way, distance - 1)).wait_send()
                across(way, distance, st, core).wait_send()


def per_device(
    features, weight, src_degree, dst_degree, cotangent, tile_rows, tile_cols, tile_count, pattern
):
    table = place_table(tile_rows, tile_cols, tile_count)
    vmem = pl.BlockSpec(memory_space=pltpu.VMEM)
    dma = pltpu.SemaphoreType.DMA
    block = (OWN, FEAT)
    scratch = [
        pltpu.VMEM((HALF, 2 * HALF), F32),
        pltpu.VMEM((COL_SPAN, FEAT), BF16),
        pltpu.VMEM((SLOTS + 1, TILE, TILE), BF16),
        pltpu.VMEM((ROW_SPAN, COL_SPAN), BF16),
        pltpu.VMEM((RING, CHUNK, FEAT), F32),
        pltpu.VMEM((RING, 2) + block, BF16),
        pltpu.VMEM((RING, 2) + block, BF16),
        pltpu.VMEM((2, 2, OWN, HALF), BF16),
        pltpu.VMEM((2, 2, OWN, HALF), BF16),
        pltpu.VMEM((2, 3, 2) + block, BF16),
        pltpu.VMEM((2, 3, 2) + block, BF16),
        pltpu.VMEM(block, BF16),
        pltpu.VMEM(block, BF16),
        pltpu.VMEM((ROW_SPAN, FEAT), BF16),
        pltpu.VMEM((FEAT, COL_SPAN), F32),
        pltpu.VMEM((COL_SPAN, FEAT), F32),
        pltpu.VMEM((COL_SPAN, FEAT), BF16),
        pltpu.VMEM((ROWS - 1,) + block, BF16),
        pltpu.VMEM((FEAT, FEAT), F32),
        pltpu.VMEM((ROWS - 1, PIECE, FEAT), F32),
        pltpu.VMEM((3, QUARTER, FEAT), F32),
        pltpu.VMEM((RING, QUARTER, FEAT), F32),
        pltpu.VMEM((FEAT, FEAT), F32),
    ]
    for shape in (
        (ROWS - 1,),
        (RING,),
        (2, 4, 2),
        (),
        (2, 4, 2),
        (2, 5, 2),
        (),
        (ROWS - 1,),
        (ROWS - 1,),
        (3,),
        (RING - 1,),
        (3,),
        (ROWS - 1,),
    ):
        scratch += [dma(shape) if shape else dma, dma(shape) if shape else dma]
    return pl.pallas_call(
        kernel,
        out_shape=(
            jax.ShapeDtypeStruct(block, BF16),
            jax.ShapeDtypeStruct(block, BF16),
            jax.ShapeDtypeStruct((FEAT, FEAT), F32),
        ),
        in_specs=[pl.BlockSpec(memory_space=pltpu.SMEM)] + [vmem] * 6,
        out_specs=(vmem, vmem, vmem),
        scratch_shapes=scratch,
        compiler_params=pltpu.CompilerParams(
            collective_id=0, has_side_effects=True, vmem_limit_bytes=60 * 1024 * 1024
        ),
        cost_estimate=pl.CostEstimate(
            flops=4 * ROW_SPAN * COL_SPAN * FEAT, bytes_accessed=3 << 20, transcendentals=0
        ),
    )(
        table,
        features,
        weight,
        src_degree.reshape(1, OWN),
        dst_degree.reshape(1, OWN),
        cotangent,
        pattern,
    )


def solution(mesh):
    placed = (
        P(("col", "row"), None),
        P(),
        P(("col", "row")),
        P(("row", "col")),
        P(("row", "col"), None),
        P(("row", "col")),
        P(("row", "col")),
        P(("row", "col")),
        P(("row", "col"), None, None),
    )
    return jax.shard_map(
        per_device,
        mesh=mesh,
        in_specs=placed,
        out_specs=(P(("row", "col"), None), P(("col", "row"), None), P()),
        check_vma=False,
    )
```

```python
import functools

import jax
import jax.numpy as jnp
from jax import lax
from jax.experimental import pallas as pl
from jax.experimental.pallas import tpu as pltpu
from jax.sharding import PartitionSpec as P

MESH = pl.DeviceIdType.MESH
F32 = jnp.float32
BF16 = jnp.bfloat16

FEAT = 256
HALF = 128
TILE = 128
SLOTS = 192
OWN = 192
ROWS = 8
RING = 8
TROWS = 48
TCOLS = 12
PLACES = TROWS * TCOLS
CHUNK = 4 * OWN
ROW_SPAN = RING * CHUNK
COL_SPAN = ROWS * OWN
PIECE = FEAT // ROWS
QUARTER = PIECE // 4
UNITS = 3
SUB = OWN // 2
TABLE_ROWS = 8


RING_PLAN = (
    (1, ((0, 0, 0), (0, 1, 1))),
    (2, ((1, 1, 0),)),
    (3, ((1, 0, 1),)),
    (4, ((1, 0, 0), (1, 1, 1), (0, 2, 0), (0, 2, 1))),
    (5, ((2, 1, 0), (2, 0, 1))),
    (6, ((2, 0, 0), (2, 1, 1), (1, 2, 0), (1, 2, 1))),
    (7, ((3, 1, 0), (3, 0, 1))),
)


def remote(src, dst, send_sem, recv_sem, device):
    return pltpu.make_async_remote_copy(
        src_ref=src,
        dst_ref=dst,
        send_sem=send_sem,
        recv_sem=recv_sem,
        device_id=device,
        device_id_type=MESH,
    )


def rows_at(start, size):
    return pl.ds(pl.multiple_of(start, 8 if size < 16 else 32), size)


def kernel(
    feat,
    weight_hbm,
    src_deg,
    dst_deg,
    cot_hbm,
    tile_rows,
    tile_cols,
    tile_count,
    pattern_hbm,
    act_out,
    hidden_out,
    w_full,
    weight,
    cot,
    pattern,
    table_vec,
    table,
    deg_buf,
    s_all,
    tiles,
    adj,
    part,
    core_out,
    core_in,
    x_out,
    x_in,
    ring_out,
    ring_in,
    xhi_out,
    xhi_in,
    sums_buf,
    grads,
    acc,
    cols_b,
    cols_in,
    w_part,
    w_out,
    w_rows,
    w_piece,
    w_quart,
    w_ring,
    load_sem,
    sent,
    w_sent,
    gat_r,
    core_r,
    x_r,
    ring_r,
    xhi_r,
    agr_r,
    agc_r,
    agx_r,
    col_r,
    w_r,
):
    r = lax.axis_index("row")
    c = lax.axis_index("col")
    z = c // 4
    quad = c % 4
    xhi = quad // 2
    core = quad % 2
    other_core = 1 - core
    other_xhi = 1 - xhi

    def row_dev(i):
        return {"row": (r + i) % ROWS}

    def quad_dev(i):
        return {"col": z * 4 + (quad + i) % 4}

    def z_dev(i):
        return {"col": ((z + i) % RING) * 4 + quad}

    core_dev = {"col": z * 4 + xhi * 2 + other_core}
    xhi_dev = {"col": z * 4 + other_xhi * 2 + core}
    ring_dev = [z_dev(1), z_dev(RING - 1)]

    loads = [
        pltpu.make_async_copy(pattern_hbm, pattern, load_sem.at[0]),
        pltpu.make_async_copy(weight_hbm, weight, load_sem.at[1]),
        pltpu.make_async_copy(cot_hbm, cot, load_sem.at[2]),
    ]
    for load in loads:
        load.start()

    barrier = pltpu.get_barrier_semaphore()

    def greet(device):
        pl.semaphore_signal(barrier, inc=1, device_id=device, device_id_type=MESH)

    def greet_rows(i, _):
        greet(row_dev(i))
        return 0

    lax.fori_loop(1, ROWS, greet_rows, 0)
    for device in (core_dev, xhi_dev, *ring_dev):
        greet(device)
    pl.semaphore_wait(barrier, ROWS - 1 + 4)

    def upright(lane_values):
        deg_buf[:, 0:OWN] = jnp.broadcast_to(lane_values, (HALF, OWN))
        return deg_buf[...].T[0:OWN, :]

    def column(deg):
        turned = upright(lax.rsqrt(deg[...].astype(F32)))
        return jnp.concatenate([turned, turned], axis=1)

    deg_buf[...] = jnp.ones_like(deg_buf)

    src_scale = column(src_deg)
    own_rows = rows_at(r * OWN, OWN)
    s_all[own_rows, :] = (feat[...].astype(F32) * src_scale).astype(BF16)

    def gather_copy(i, sender):
        span = rows_at(sender * OWN, OWN)
        return remote(s_all.at[span], s_all.at[span], sent, gat_r, row_dev(i))

    def gather_start(i, _):
        gather_copy(i, r).start()
        return 0

    lax.fori_loop(1, ROWS, gather_start, 0)

    lane = lax.broadcasted_iota(jnp.int32, (1, OWN), 1)
    place = jnp.where(lane < tile_count[0], tile_rows[...] * TCOLS + tile_cols[...], -1)
    place_down = upright(place.astype(F32)).astype(jnp.int32)
    slot_down = lax.broadcasted_iota(jnp.int32, (SLOTS, TILE), 0)
    lanes = lax.broadcasted_iota(jnp.int32, (SLOTS, TILE), 1)

    def last_slot(named):
        last = jnp.max(jnp.where(named, slot_down, -1), axis=0, keepdims=True)
        return jnp.where(last < 0, SLOTS, last)

    table_vec[...] = jnp.full_like(table_vec, SLOTS)
    for row in range(5):
        table_vec[row : row + 1, :] = last_slot(place_down == lanes + row * TILE)
    for row, start, size in ((5, 0, TILE), (6, TILE, SLOTS - TILE)):
        asked = place[:, start : start + size]
        if size < TILE:
            asked = jnp.concatenate([asked, jnp.full((1, TILE - size), -2, jnp.int32)], axis=1)
        named = (place_down == asked) & (slot_down < lanes + start) & (place_down >= 0)
        table_vec[row : row + 1, :] = last_slot(named)
    to_smem = pltpu.make_async_copy(table_vec, table, load_sem.at[3])
    to_smem.start()
    to_smem.wait()
    loads[0].wait()

    tiles[SLOTS] = jnp.zeros((TILE, TILE), BF16)
    bit = lax.broadcasted_iota(jnp.int32, (TILE // 8, 8, TILE), 1)

    def unpack(k, _):
        words = jnp.broadcast_to(pattern[k][:, None, :], (TILE // 8, 8, TILE))
        bits = jnp.bitwise_and(jnp.right_shift(words, bit), 1).reshape(TILE, TILE)
        tiles[k] = bits.astype(F32).astype(BF16) + tiles[table[5 + k // TILE, k % TILE]]
        return 0

    lax.fori_loop(0, SLOTS, unpack, 0)

    def assemble(t, _):
        for j in range(TCOLS):
            at = t * TCOLS + j
            adj[rows_at(t * TILE, TILE), j * TILE : (j + 1) * TILE] = tiles[
                table[at // TILE, at % TILE]
            ]
        return 0

    lax.fori_loop(0, TROWS, assemble, 0)

    def arrived_all(ref, sem):
        pltpu.make_async_copy(ref, ref, sem).wait()

    arrived_all(s_all.at[pl.ds(0, COL_SPAN - OWN)], gat_r)

    def core_copy(i):
        return remote(core_out.at[i], core_in.at[i], sent, core_r.at[i], core_dev)

    LOW, HIGH = slice(0, HALF), slice(HALF, FEAT)

    def core_sum(i, xh, lanes):
        mine = part[i, rows_at((2 * xh + core) * OWN, OWN), lanes]
        return mine + core_in[i, xh, :, lanes].astype(F32)

    def x_copy(i):
        return remote(x_out.at[i], x_in.at[i], sent, x_r.at[i], xhi_dev)

    def x_wait(i):
        x_copy(i).wait_recv()

    def merge(i):
        core_copy(i).wait_recv()
        x_out[i] = core_sum(i, other_xhi, HIGH).astype(BF16)
        x_copy(i).start()

    def unit_sum(i, unit):
        if unit < 2:
            return core_sum(i, (other_xhi, xhi)[unit], LOW)
        return core_sum(i, xhi, HIGH) + x_in[i].astype(F32)

    def ring_rows(way, step, unit):
        if step > 0:
            return slice(0, OWN)
        if unit < 2:
            return slice(0, OWN) if unit == way else None
        return slice(way * SUB, (way + 1) * SUB)

    def ring_copy(way, step, unit):
        rows = ring_rows(way, step, unit)
        rows = pl.ds(rows.start, rows.stop - rows.start)
        return remote(
            ring_out.at[way, step, unit, rows],
            ring_in.at[way, step, unit, rows],
            sent,
            ring_r.at[way, step, unit],
            ring_dev[way],
        )

    def ring_step(step, unit, way):
        rows = ring_rows(way, step, unit)
        if step == 0:
            ring_out[way, 0, unit, rows, :] = unit_sum(0, unit)[rows].astype(BF16)
            ring_copy(way, 0, unit).start()
            return
        total = unit_sum(2 * step - 1 + way, unit)
        arrived = ring_rows(way, step - 1, unit)
        if arrived is None:
            ring_out[way, step, unit] = total.astype(BF16)
        else:
            ring_copy(way, step - 1, unit).wait_recv()
            for half in (slice(0, SUB), slice(SUB, OWN)):
                block = total[half]
                if arrived.start <= half.start and half.stop <= arrived.stop:
                    block = block + ring_in[way, step - 1, unit, half, :].astype(F32)
                ring_out[way, step, unit, half, :] = block.astype(BF16)
        ring_copy(way, step, unit).start()

    def home_sum(unit):
        total = unit_sum(7, unit)
        for way in range(2):
            ring_copy(way, 3, unit).wait_recv()
            total = total + ring_in[way, 3, unit].astype(F32)
        return total

    def forward_chunk(i, _):
        back = 4 - (i + 1) // 2
        there = (z + jnp.where(i % 2 == 1, back, RING - back)) % RING
        part[i] = jnp.dot(
            adj[rows_at(there * CHUNK, CHUNK), :], s_all[...], preferred_element_type=F32
        )
        for xh in range(2):
            theirs = part[i, rows_at((2 * xh + other_core) * OWN, OWN), :]
            core_out[i, xh] = theirs.astype(BF16)
        core_copy(i).start()
        pl.when(i > 0)(functools.partial(merge, i - 1))
        for at, steps in RING_PLAN:
            for step, unit, way in steps:
                if unit == 2 and (step > 0 or way == 0):
                    slot = 2 * step - 1 + way if step else 0
                    pl.when(i == at)(functools.partial(x_wait, slot))
                pl.when(i == at)(functools.partial(ring_step, step, unit, way))
        return 0

    lax.fori_loop(0, RING, forward_chunk, 0)

    merge(7)
    ring_step(3, 0, 0)
    ring_step(3, 1, 1)
    for way in range(2):
        x_copy(3 + way).wait_recv()
        ring_step(2, 2, way)
    xhi_out[...] = home_sum(0).astype(BF16)
    xhi_copy = remote(xhi_out, xhi_in, sent, xhi_r, xhi_dev)
    xhi_copy.start()
    for way in range(2):
        x_copy(5 + way).wait_recv()
        ring_step(3, 2, way)
    x_copy(7).wait_recv()
    sums_buf[:, LOW] = home_sum(1)
    loads[1].wait()
    loads[2].wait()
    dst_scale = column(dst_deg)
    sums_buf[:, HIGH] = home_sum(2)
    xhi_copy.wait_recv()
    sums_buf[:, LOW] += xhi_in[...].astype(F32)
    sums = sums_buf[...]

    high = sums.astype(BF16)
    low = (sums - high.astype(F32)).astype(BF16)

    def preact_of(lanes):
        mixed = jnp.dot(high, weight[:, lanes], preferred_element_type=F32)
        mixed = mixed + jnp.dot(low, weight[:, lanes], preferred_element_type=F32)
        return dst_scale[:, lanes] * mixed

    def decay_of(preact):
        return jnp.exp(jnp.minimum(preact, 0.0))

    grad_rows = rows_at(z * CHUNK + quad * OWN, OWN)

    def put_grads(lanes):
        preact = preact_of(lanes)
        decay = decay_of(preact)
        slope = jnp.where(preact > 0, 1.0, decay)
        grads[grad_rows, lanes] = (
            dst_scale[:, lanes] * (cot[:, lanes].astype(F32) * slope)
        ).astype(BF16)
        act_out[:, lanes] = jnp.where(preact > 0, preact, decay - 1.0).astype(BF16)


    def origin(way, distance):
        return (z + (RING - distance if way == 0 else distance)) % RING

    def block(chip, distance, way, unit, cr):
        xh = xhi if unit < 2 else other_xhi
        start, size = 0, OWN
        if distance == 4 and unit in (0, 3):
            start, size = way * SUB, SUB
        rows = rows_at(chip * CHUNK + (2 * xh + cr) * OWN + start, size)
        return grads.at[rows, pl.ds(0 if unit in (1, 2) else HALF, HALF)]

    def ways(distance, unit):
        if distance == 0:
            return (0,)
        if distance == 4 and unit in (1, 2):
            return (unit - 1,)
        return (0, 1)

    def around(way, distance, unit, chip):
        ref = block(chip, distance, way, unit, core)
        return remote(ref, ref, sent, agr_r.at[way, distance - 1, unit], ring_dev[way])

    def across(way, distance, unit, cr):
        ref = block(origin(way, distance), distance, way, unit, cr)
        return remote(ref, ref, sent, agc_r.at[distance, 0 if distance == 4 else way], core_dev)

    def over(way, distance, unit):
        at = distance if unit in (0, 3) else 5
        ref = block(origin(way, distance), distance, way, unit, core)
        return remote(ref, ref, sent, agx_r.at[way, at], xhi_dev)

    put_grads(LOW)
    over(0, 0, 1).start()
    put_grads(HIGH)
    for way in range(2):
        around(way, 1, 0, z).start()
    over(0, 0, 0).start()
    for unit in range(2):
        across(0, 0, unit, core).start()

    turn = (((0,), (0,)), ((), ()))
    grad_own = grads[grad_rows, :]
    w_part[...] = lax.dot_general(high, grad_own, turn, preferred_element_type=F32)
    w_part[...] += lax.dot_general(low, grad_own, turn, preferred_element_type=F32)
    w_out[...] = w_part[...].astype(BF16)

    def w1_copy(i):
        mine = w_out.at[rows_at(((r + i) % ROWS) * PIECE, PIECE)]
        return remote(mine, w_rows.at[i - 1], w_sent, w_r.at[0], row_dev(i))

    def w2_copy(i):
        start = r * PIECE + ((quad + i) % 4) * QUARTER
        mine = w_part.at[rows_at(start, QUARTER)]
        return remote(mine, w_quart.at[i - 1], w_sent, w_r.at[1], quad_dev(i))

    def w3_copy(i, sender):
        return remote(
            w_ring.at[sender], w_ring.at[sender], w_sent, w_r.at[2], z_dev(i)
        )

    def w4_copy(i, sender):
        ref = w_piece.at[rows_at(sender * QUARTER, QUARTER)]
        return remote(ref, ref, w_sent, w_r.at[3], quad_dev(i))

    def w5_copy(i, sender):
        ref = w_full.at[rows_at(sender * PIECE, PIECE)]
        return remote(ref, ref, w_sent, w_r.at[4], row_dev(i))

    def each(count, action):
        def body(i, _):
            action(i)
            return 0

        lax.fori_loop(1, count, body, 0)

    def w_stage1():
        each(ROWS, lambda i: w1_copy(i).start())

    def w_stage2():
        arrived_all(w_rows, w_r.at[0])
        piece = rows_at(r * PIECE, PIECE)
        total = w_part[piece, :]
        for i in range(ROWS - 1):
            total = total + w_rows[i].astype(F32)
        w_part[piece, :] = total
        each(4, lambda i: w2_copy(i).start())

    def w_stage3():
        arrived_all(w_quart, w_r.at[1])
        total = w_part[rows_at(r * PIECE + quad * QUARTER, QUARTER), :]
        for i in range(3):
            total = total + w_quart[i]
        w_ring[z] = total
        each(RING, lambda i: w3_copy(i, z).start())

    def w_stage4():
        arrived_all(w_ring.at[pl.ds(0, RING - 1)], w_r.at[2])
        total = w_ring[0]
        for i in range(1, RING):
            total = total + w_ring[i]
        w_piece[rows_at(quad * QUARTER, QUARTER), :] = total
        each(4, lambda i: w4_copy(i, quad).start())

    def w_stage5():
        arrived_all(w_piece.at[pl.ds(0, 3 * QUARTER)], w_r.at[3])
        w_full[rows_at(r * PIECE, PIECE), :] = w_piece[...].astype(BF16)
        each(ROWS, lambda i: w5_copy(i, r).start())

    w_stage1()

    for way in range(2):
        around(way, 1, 1, z).start()
    over(0, 0, 2).wait_recv()
    for way in range(2):
        around(way, 1, 2, z).start()
    across(0, 0, 2, core).start()

    acc[...] = jnp.zeros_like(acc)

    def arrive(distance, unit):
        for way in ways(distance, unit):
            chip = origin(way, distance)
            around(way, distance, unit, chip).wait_recv()
            if distance < 4 and way in ways(distance + 1, unit):
                around(way, distance + 1, unit, chip).start()
            across(way, distance, unit, core).start()
            if unit == 0:
                over(way, distance, 0).start()

    def arrive_over(distance):
        for way in ways(distance, 3):
            over(way, distance, 3).wait_recv()
            across(way, distance, 3, core).start()

    def cross_wait(distance, way):
        arrived_all(grads.at[pl.ds(0, 2 * OWN)], agc_r.at[distance, way])

    def ahead(i):
        if i == 0:
            arrive(1, 0)
            arrive_over(0)
            arrive(1, 1)
            cross_wait(0, 0)
        elif i < 7:
            distance, way = (i + 1) // 2, (i + 1) % 2
            if way == 0:
                if distance == 1:
                    arrive(2, 0)
                arrive(distance, 2)
                arrive_over(distance)
                arrive(distance + 1, 1)
            elif distance < 3:
                arrive(distance + 2, 0)
            cross_wait(distance, way)
        else:
            arrive(4, 2)
            arrive_over(4)
            cross_wait(4, 0)

    def backward_chunk(i, _):
        for at in range(RING):
            pl.when(i == at)(functools.partial(ahead, at))
        away = (i + 1) // 2
        there = (z + jnp.where(i % 2 == 1, RING - away, away)) % RING
        span = rows_at(there * CHUNK, CHUNK)
        acc[...] += lax.dot_general(
            adj[span, :], grads[span, :], turn, preferred_element_type=F32
        )
        pl.when(i == 2)(w_stage2)
        pl.when(i == 4)(w_stage3)
        pl.when(i == 6)(w_stage4)
        return 0

    lax.fori_loop(0, RING, backward_chunk, 0)

    cols_b[...] = acc[...].astype(BF16)

    def col_copy(i):
        mine = cols_b.at[rows_at(((r + i) % ROWS) * OWN, OWN)]
        return remote(mine, cols_in.at[i - 1], sent, col_r, row_dev(i))

    each(ROWS, lambda i: col_copy(i).start())
    w_stage5()

    arrived_all(w_full.at[pl.ds(0, FEAT - PIECE)], w_r.at[4])
    src_again = column(src_deg)
    arrived_all(cols_in, col_r)
    total = acc[own_rows, :]
    for i in range(ROWS - 1):
        total = total + cols_in[i].astype(F32)
    hidden_out[...] = (src_again * total).astype(BF16)

    blocks = 2 * 14 + 2 * 32 + 18 + 2 * 21
    arrived_all(adj.at[pl.ds(0, blocks * OWN * HALF // COL_SPAN)], sent)
    w_rows_sent = 14 * PIECE // 2 + 13 * QUARTER
    arrived_all(part.at[0, pl.ds(0, w_rows_sent)], w_sent)


def finish(act, hidden, weight, w_sum, act_out, gf_out, gw_out):
    act_out[...] = act[...]
    gf_out[...] = lax.dot_general(
        hidden[...], weight[...], (((1,), (1,)), ((), ())), preferred_element_type=F32
    ).astype(BF16)
    full = w_sum[...].astype(F32)
    root = jnp.sqrt(jnp.sum(full * full) * (1.0 / (FEAT * FEAT)))
    gw_out[...] = full * jnp.minimum(1.0, 1.0 / (root + 1e-6))


def per_device(
    features, weight, src_degree, dst_degree, cotangent, tile_rows, tile_cols, tile_count, pattern
):
    vmem = pl.BlockSpec(memory_space=pltpu.VMEM)
    smem = pl.BlockSpec(memory_space=pltpu.SMEM)
    hbm = pl.BlockSpec(memory_space=pl.ANY)
    dma = pltpu.SemaphoreType.DMA
    block = (OWN, FEAT)
    scratch = [
        pltpu.VMEM((FEAT, FEAT), BF16),
        pltpu.VMEM(block, BF16),
        pltpu.VMEM((SLOTS, TILE // 8, TILE), jnp.int32),
        pltpu.VMEM((TABLE_ROWS, TILE), jnp.int32),
        pltpu.SMEM((TABLE_ROWS, TILE), jnp.int32),
        pltpu.VMEM((HALF, 2 * HALF), F32),
        pltpu.VMEM((COL_SPAN, FEAT), BF16),
        pltpu.VMEM((SLOTS + 1, TILE, TILE), BF16),
        pltpu.VMEM((ROW_SPAN, COL_SPAN), BF16),
        pltpu.VMEM((RING, CHUNK, FEAT), F32),
        pltpu.VMEM((RING, 2) + block, BF16),
        pltpu.VMEM((RING, 2) + block, BF16),
        pltpu.VMEM((RING, OWN, HALF), BF16),
        pltpu.VMEM((RING, OWN, HALF), BF16),
        pltpu.VMEM((2, 4, UNITS, OWN, HALF), BF16),
        pltpu.VMEM((2, 4, UNITS, OWN, HALF), BF16),
        pltpu.VMEM((OWN, HALF), BF16),
        pltpu.VMEM((OWN, HALF), BF16),
        pltpu.VMEM(block, F32),
        pltpu.VMEM((ROW_SPAN, FEAT), BF16),
        pltpu.VMEM((COL_SPAN, FEAT), F32),
        pltpu.VMEM((COL_SPAN, FEAT), BF16),
        pltpu.VMEM((ROWS - 1,) + block, BF16),
        pltpu.VMEM((FEAT, FEAT), F32),
        pltpu.VMEM((FEAT, FEAT), BF16),
        pltpu.VMEM((ROWS - 1, PIECE, FEAT), BF16),
        pltpu.VMEM((PIECE, FEAT), F32),
        pltpu.VMEM((3, QUARTER, FEAT), F32),
        pltpu.VMEM((RING, QUARTER, FEAT), F32),
        dma((4,)),
    ]
    scratch += [
        dma,
        dma,
        dma,
        dma((RING,)),
        dma((RING,)),
        dma((2, 4, UNITS)),
        dma,
        dma((2, 4, UNITS)),
        dma((5, 2)),
        dma((2, 6)),
        dma,
        dma((5,)),
    ]
    act, hidden, w_sum = pl.pallas_call(
        kernel,
        out_shape=(
            jax.ShapeDtypeStruct(block, BF16),
            jax.ShapeDtypeStruct(block, BF16),
            jax.ShapeDtypeStruct((FEAT, FEAT), BF16),
        ),
        in_specs=[vmem, hbm, vmem, vmem, hbm, vmem, vmem, smem, hbm],
        out_specs=(vmem, vmem, vmem),
        scratch_shapes=scratch,
        compiler_params=pltpu.CompilerParams(
            collective_id=0, has_side_effects=True, vmem_limit_bytes=60 * 1024 * 1024
        ),
        cost_estimate=pl.CostEstimate(
            flops=4 * ROW_SPAN * COL_SPAN * FEAT, bytes_accessed=3 << 20, transcendentals=0
        ),
    )(
        features,
        weight,
        src_degree.reshape(1, OWN),
        dst_degree.reshape(1, OWN),
        cotangent,
        tile_rows.reshape(1, OWN),
        tile_cols.reshape(1, OWN),
        tile_count,
        pattern,
    )
    return pl.pallas_call(
        finish,
        out_shape=(
            jax.ShapeDtypeStruct(block, BF16),
            jax.ShapeDtypeStruct(block, BF16),
            jax.ShapeDtypeStruct((FEAT, FEAT), F32),
        ),
        in_specs=[vmem] * 4,
        out_specs=(vmem, vmem, vmem),
    )(act, hidden, weight, w_sum)


def solution(mesh):
    placed = (
        P(("col", "row"), None),
        P(),
        P(("col", "row")),
        P(("row", "col")),
        P(("row", "col"), None),
        P(("row", "col")),
        P(("row", "col")),
        P(("row", "col")),
        P(("row", "col"), None, None),
    )
    return jax.shard_map(
        per_device,
        mesh=mesh,
        in_specs=placed,
        out_specs=(P(("row", "col"), None), P(("col", "row"), None), P()),
        check_vma=False,
    )
```

```python
import functools

import jax
import jax.numpy as jnp
from jax import lax
from jax.experimental import pallas as pl
from jax.experimental.pallas import tpu as pltpu
from jax.sharding import PartitionSpec as P

MESH = pl.DeviceIdType.MESH
F32 = jnp.float32
BF16 = jnp.bfloat16

FEAT = 256
HALF = 128
TILE = 128
SLOTS = 192
OWN = 192
ROWS = 8
RING = 8
TROWS = 48
TCOLS = 12
PLACES = TROWS * TCOLS
CHUNK = 4 * OWN
ROW_SPAN = RING * CHUNK
COL_SPAN = ROWS * OWN
PIECE = FEAT // ROWS
QUARTER = PIECE // 4
UNITS = 3
SUB = OWN // 2
TABLE_ROWS = 8
UNROLL = 4


RING_PLAN = (
    (1, ((0, 0, 0), (0, 1, 1))),
    (2, ((1, 1, 0),)),
    (3, ((1, 0, 1),)),
    (4, ((1, 0, 0), (1, 1, 1), (0, 2, 0), (0, 2, 1))),
    (5, ((2, 1, 0), (2, 0, 1))),
    (6, ((2, 0, 0), (2, 1, 1), (1, 2, 0), (1, 2, 1))),
    (7, ((3, 1, 0), (3, 0, 1))),
)


def remote(src, dst, send_sem, recv_sem, device):
    return pltpu.make_async_remote_copy(
        src_ref=src,
        dst_ref=dst,
        send_sem=send_sem,
        recv_sem=recv_sem,
        device_id=device,
        device_id_type=MESH,
    )


def rows_at(start, size):
    return pl.ds(pl.multiple_of(start, 8 if size < 16 else 32), size)


def kernel(
    feat,
    weight_hbm,
    src_deg,
    dst_deg,
    cot_hbm,
    tile_rows,
    tile_cols,
    tile_count,
    pattern_hbm,
    act_out,
    hidden_out,
    w_full,
    weight,
    cot,
    pattern,
    table_vec,
    table,
    deg_buf,
    s_all,
    tiles,
    adj,
    part,
    core_out,
    core_in,
    x_out,
    x_in,
    ring_out,
    ring_in,
    xhi_out,
    xhi_in,
    sums_buf,
    grads,
    acc,
    cols_b,
    cols_in,
    w_part,
    w_out,
    w_rows,
    w_piece,
    w_quart,
    w_ring,
    load_sem,
    sent,
    w_sent,
    gat_r,
    core_r,
    x_r,
    ring_r,
    xhi_r,
    agr_r,
    agc_r,
    agx_r,
    col_r,
    w_r,
):
    r = lax.axis_index("row")
    c = lax.axis_index("col")
    z = c // 4
    quad = c % 4
    xhi = quad // 2
    core = quad % 2
    other_core = 1 - core
    other_xhi = 1 - xhi

    def row_dev(i):
        return {"row": (r + i) % ROWS}

    def quad_dev(i):
        return {"col": z * 4 + (quad + i) % 4}

    def z_dev(i):
        return {"col": ((z + i) % RING) * 4 + quad}

    core_dev = {"col": z * 4 + xhi * 2 + other_core}
    xhi_dev = {"col": z * 4 + other_xhi * 2 + core}
    ring_dev = [z_dev(1), z_dev(RING - 1)]

    loads = [
        pltpu.make_async_copy(pattern_hbm, pattern, load_sem.at[0]),
        pltpu.make_async_copy(weight_hbm, weight, load_sem.at[1]),
        pltpu.make_async_copy(cot_hbm, cot, load_sem.at[2]),
    ]
    for load in loads:
        load.start()

    barrier = pltpu.get_barrier_semaphore()

    def greet(device):
        pl.semaphore_signal(barrier, inc=1, device_id=device, device_id_type=MESH)

    def greet_rows(i, _):
        greet(row_dev(i))
        return 0

    lax.fori_loop(1, ROWS, greet_rows, 0)
    for device in (core_dev, xhi_dev, *ring_dev):
        greet(device)
    def upright(lane_values):
        deg_buf[:, 0:OWN] = jnp.broadcast_to(lane_values, (HALF, OWN))
        return deg_buf[...].T[0:OWN, :]

    def column(deg):
        turned = upright(lax.rsqrt(deg[...].astype(F32)))
        return jnp.concatenate([turned, turned], axis=1)

    deg_buf[...] = jnp.ones_like(deg_buf)

    src_scale = column(src_deg)
    own_rows = rows_at(r * OWN, OWN)
    s_all[own_rows, :] = (feat[...].astype(F32) * src_scale).astype(BF16)

    lane = lax.broadcasted_iota(jnp.int32, (1, OWN), 1)
    place = jnp.where(lane < tile_count[0], tile_rows[...] * TCOLS + tile_cols[...], -1)
    place_down = upright(place.astype(F32)).astype(jnp.int32)
    slot_down = lax.broadcasted_iota(jnp.int32, (SLOTS, TILE), 0)
    lanes = lax.broadcasted_iota(jnp.int32, (SLOTS, TILE), 1)

    def last_slot(named):
        last = jnp.max(jnp.where(named, slot_down, -1), axis=0, keepdims=True)
        return jnp.where(last < 0, SLOTS, last)

    for row in range(TROWS // 8):
        asked = (row * 8 + lanes // 16) * TCOLS + lanes % 16
        named = (place_down == asked) & (lanes % 16 < TCOLS)
        table_vec[row : row + 1, :] = last_slot(named)
    for row, start, size in ((6, 0, TILE), (7, TILE, SLOTS - TILE)):
        asked = place[:, start : start + size]
        if size < TILE:
            asked = jnp.concatenate([asked, jnp.full((1, TILE - size), -2, jnp.int32)], axis=1)
        named = (place_down == asked) & (slot_down < lanes + start) & (place_down >= 0)
        table_vec[row : row + 1, :] = last_slot(named)
    to_smem = pltpu.make_async_copy(table_vec, table, load_sem.at[3])
    to_smem.start()

    pl.semaphore_wait(barrier, ROWS - 1 + 4)

    def gather_copy(i, sender):
        span = rows_at(sender * OWN, OWN)
        return remote(s_all.at[span], s_all.at[span], sent, gat_r, row_dev(i))

    def gather_start(i, _):
        gather_copy(i, r).start()
        return 0

    lax.fori_loop(1, ROWS, gather_start, 0)

    to_smem.wait()
    loads[0].wait()

    tiles[SLOTS] = jnp.zeros((TILE, TILE), BF16)
    bit = lax.broadcasted_iota(jnp.int32, (TILE // 8, 8, TILE), 1)

    def unpack(row, first):
        def one(k, _):
            words = jnp.broadcast_to(pattern[first + k][:, None, :], (TILE // 8, 8, TILE))
            bits = jnp.bitwise_and(jnp.right_shift(words, bit), 1).reshape(TILE, TILE)
            tiles[first + k] = bits.astype(F32).astype(BF16) + tiles[table[row, k]]
            return 0

        return one

    lax.fori_loop(0, TILE, unpack(6, 0), 0, unroll=UNROLL)
    lax.fori_loop(0, SLOTS - TILE, unpack(7, TILE), 0, unroll=UNROLL)

    def assemble(row, _):
        for t in range(8):
            for j in range(TCOLS):
                adj[rows_at((row * 8 + t) * TILE, TILE), j * TILE : (j + 1) * TILE] = tiles[
                    table[row, t * 16 + j]
                ]
        return 0

    lax.fori_loop(0, TROWS // 8, assemble, 0)

    def arrived_all(ref, sem):
        pltpu.make_async_copy(ref, ref, sem).wait()

    arrived_all(s_all.at[pl.ds(0, COL_SPAN - OWN)], gat_r)

    def core_copy(i):
        return remote(core_out.at[i], core_in.at[i], sent, core_r.at[i], core_dev)

    LOW, HIGH = slice(0, HALF), slice(HALF, FEAT)

    def core_sum(i, xh, lanes):
        mine = part[i, rows_at((2 * xh + core) * OWN, OWN), lanes]
        return mine + core_in[i, xh, :, lanes].astype(F32)

    def x_copy(i):
        return remote(x_out.at[i], x_in.at[i], sent, x_r.at[i], xhi_dev)

    def x_wait(i):
        x_copy(i).wait_recv()

    def merge(i):
        core_copy(i).wait_recv()
        x_out[i] = core_sum(i, other_xhi, HIGH).astype(BF16)
        x_copy(i).start()

    def unit_sum(i, unit):
        if unit < 2:
            return core_sum(i, (other_xhi, xhi)[unit], LOW)
        return core_sum(i, xhi, HIGH) + x_in[i].astype(F32)

    def ring_rows(way, step, unit):
        if step > 0:
            return slice(0, OWN)
        if unit < 2:
            return slice(0, OWN) if unit == way else None
        return slice(way * SUB, (way + 1) * SUB)

    def ring_copy(way, step, unit):
        rows = ring_rows(way, step, unit)
        rows = pl.ds(rows.start, rows.stop - rows.start)
        return remote(
            ring_out.at[way, step, unit, rows],
            ring_in.at[way, step, unit, rows],
            sent,
            ring_r.at[way, step, unit],
            ring_dev[way],
        )

    def ring_step(step, unit, way):
        rows = ring_rows(way, step, unit)
        if step == 0:
            ring_out[way, 0, unit, rows, :] = unit_sum(0, unit)[rows].astype(BF16)
            ring_copy(way, 0, unit).start()
            return
        total = unit_sum(2 * step - 1 + way, unit)
        arrived = ring_rows(way, step - 1, unit)
        if arrived is None:
            ring_out[way, step, unit] = total.astype(BF16)
        else:
            ring_copy(way, step - 1, unit).wait_recv()
            for half in (slice(0, SUB), slice(SUB, OWN)):
                block = total[half]
                if arrived.start <= half.start and half.stop <= arrived.stop:
                    block = block + ring_in[way, step - 1, unit, half, :].astype(F32)
                ring_out[way, step, unit, half, :] = block.astype(BF16)
        ring_copy(way, step, unit).start()

    def home_sum(unit):
        total = unit_sum(7, unit)
        for way in range(2):
            ring_copy(way, 3, unit).wait_recv()
            total = total + ring_in[way, 3, unit].astype(F32)
        return total

    def forward_chunk(i, _):
        back = 4 - (i + 1) // 2
        there = (z + jnp.where(i % 2 == 1, back, RING - back)) % RING
        part[i] = jnp.dot(
            adj[rows_at(there * CHUNK, CHUNK), :], s_all[...], preferred_element_type=F32
        )
        for xh in range(2):
            theirs = part[i, rows_at((2 * xh + other_core) * OWN, OWN), :]
            core_out[i, xh] = theirs.astype(BF16)
        core_copy(i).start()
        pl.when(i > 0)(functools.partial(merge, i - 1))
        for at, steps in RING_PLAN:
            for step, unit, way in steps:
                if unit == 2 and (step > 0 or way == 0):
                    slot = 2 * step - 1 + way if step else 0
                    pl.when(i == at)(functools.partial(x_wait, slot))
                pl.when(i == at)(functools.partial(ring_step, step, unit, way))
        return 0

    lax.fori_loop(0, RING, forward_chunk, 0)

    merge(7)
    ring_step(3, 0, 0)
    ring_step(3, 1, 1)
    for way in range(2):
        x_copy(3 + way).wait_recv()
        ring_step(2, 2, way)
    xhi_out[...] = home_sum(0).astype(BF16)
    xhi_copy = remote(xhi_out, xhi_in, sent, xhi_r, xhi_dev)
    xhi_copy.start()
    for way in range(2):
        x_copy(5 + way).wait_recv()
        ring_step(3, 2, way)
    x_copy(7).wait_recv()
    sums_buf[:, LOW] = home_sum(1)
    loads[1].wait()
    loads[2].wait()
    dst_scale = column(dst_deg)
    sums_buf[:, HIGH] = home_sum(2)
    xhi_copy.wait_recv()
    sums_buf[:, LOW] += xhi_in[...].astype(F32)
    sums = sums_buf[...]

    high = sums.astype(BF16)
    low = (sums - high.astype(F32)).astype(BF16)

    def preact_of(lanes):
        mixed = jnp.dot(high, weight[:, lanes], preferred_element_type=F32)
        mixed = mixed + jnp.dot(low, weight[:, lanes], preferred_element_type=F32)
        return dst_scale[:, lanes] * mixed

    def decay_of(preact):
        return jnp.exp(jnp.minimum(preact, 0.0))

    grad_rows = rows_at(z * CHUNK + quad * OWN, OWN)

    def put_grads(lanes):
        preact = preact_of(lanes)
        decay = decay_of(preact)
        slope = jnp.where(preact > 0, 1.0, decay)
        grads[grad_rows, lanes] = (
            dst_scale[:, lanes] * (cot[:, lanes].astype(F32) * slope)
        ).astype(BF16)
        act_out[:, lanes] = jnp.where(preact > 0, preact, decay - 1.0).astype(BF16)


    def origin(way, distance):
        return (z + (RING - distance if way == 0 else distance)) % RING

    def block(chip, distance, way, unit, cr):
        xh = xhi if unit < 2 else other_xhi
        start, size = 0, OWN
        if distance == 4 and unit in (0, 3):
            start, size = way * SUB, SUB
        rows = rows_at(chip * CHUNK + (2 * xh + cr) * OWN + start, size)
        return grads.at[rows, pl.ds(0 if unit in (1, 2) else HALF, HALF)]

    def ways(distance, unit):
        if distance == 0:
            return (0,)
        if distance == 4 and unit in (1, 2):
            return (unit - 1,)
        return (0, 1)

    def around(way, distance, unit, chip):
        ref = block(chip, distance, way, unit, core)
        return remote(ref, ref, sent, agr_r.at[way, distance - 1, unit], ring_dev[way])

    def across(way, distance, unit, cr):
        ref = block(origin(way, distance), distance, way, unit, cr)
        return remote(ref, ref, sent, agc_r.at[distance, 0 if distance == 4 else way], core_dev)

    def over(way, distance, unit):
        at = distance if unit in (0, 3) else 5
        ref = block(origin(way, distance), distance, way, unit, core)
        return remote(ref, ref, sent, agx_r.at[way, at], xhi_dev)

    put_grads(LOW)
    over(0, 0, 1).start()
    put_grads(HIGH)
    for way in range(2):
        around(way, 1, 0, z).start()
    over(0, 0, 0).start()
    for unit in range(2):
        across(0, 0, unit, core).start()

    turn = (((0,), (0,)), ((), ()))
    grad_own = grads[grad_rows, :]
    w_part[...] = lax.dot_general(high, grad_own, turn, preferred_element_type=F32)
    w_part[...] += lax.dot_general(low, grad_own, turn, preferred_element_type=F32)
    w_out[...] = w_part[...].astype(BF16)

    def w1_copy(i):
        mine = w_out.at[rows_at(((r + i) % ROWS) * PIECE, PIECE)]
        return remote(mine, w_rows.at[i - 1], w_sent, w_r.at[0], row_dev(i))

    def w2_copy(i):
        start = r * PIECE + ((quad + i) % 4) * QUARTER
        mine = w_part.at[rows_at(start, QUARTER)]
        return remote(mine, w_quart.at[i - 1], w_sent, w_r.at[1], quad_dev(i))

    def w3_copy(i, sender):
        return remote(
            w_ring.at[sender], w_ring.at[sender], w_sent, w_r.at[2], z_dev(i)
        )

    def w4_copy(i, sender):
        ref = w_piece.at[rows_at(sender * QUARTER, QUARTER)]
        return remote(ref, ref, w_sent, w_r.at[3], quad_dev(i))

    def w5_copy(i, sender):
        ref = w_full.at[rows_at(sender * PIECE, PIECE)]
        return remote(ref, ref, w_sent, w_r.at[4], row_dev(i))

    def each(count, action):
        def body(i, _):
            action(i)
            return 0

        lax.fori_loop(1, count, body, 0)

    def w_stage1():
        each(ROWS, lambda i: w1_copy(i).start())

    def w_stage2():
        arrived_all(w_rows, w_r.at[0])
        piece = rows_at(r * PIECE, PIECE)
        total = w_part[piece, :]
        for i in range(ROWS - 1):
            total = total + w_rows[i].astype(F32)
        w_part[piece, :] = total
        each(4, lambda i: w2_copy(i).start())

    def w_stage3():
        arrived_all(w_quart, w_r.at[1])
        total = w_part[rows_at(r * PIECE + quad * QUARTER, QUARTER), :]
        for i in range(3):
            total = total + w_quart[i]
        w_ring[z] = total
        each(RING, lambda i: w3_copy(i, z).start())

    def w_stage4():
        arrived_all(w_ring.at[pl.ds(0, RING - 1)], w_r.at[2])
        total = w_ring[0]
        for i in range(1, RING):
            total = total + w_ring[i]
        w_piece[rows_at(quad * QUARTER, QUARTER), :] = total
        each(4, lambda i: w4_copy(i, quad).start())

    def w_stage5():
        arrived_all(w_piece.at[pl.ds(0, 3 * QUARTER)], w_r.at[3])
        w_full[rows_at(r * PIECE, PIECE), :] = w_piece[...].astype(BF16)
        each(ROWS, lambda i: w5_copy(i, r).start())

    w_stage1()

    for way in range(2):
        around(way, 1, 1, z).start()
    over(0, 0, 2).wait_recv()
    for way in range(2):
        around(way, 1, 2, z).start()
    across(0, 0, 2, core).start()

    acc[...] = jnp.zeros_like(acc)

    def arrive(distance, unit):
        for way in ways(distance, unit):
            chip = origin(way, distance)
            around(way, distance, unit, chip).wait_recv()
            if distance < 4 and way in ways(distance + 1, unit):
                around(way, distance + 1, unit, chip).start()
            across(way, distance, unit, core).start()
            if unit == 0:
                over(way, distance, 0).start()

    def arrive_over(distance):
        for way in ways(distance, 3):
            over(way, distance, 3).wait_recv()
            across(way, distance, 3, core).start()

    def cross_wait(distance, way):
        arrived_all(grads.at[pl.ds(0, 2 * OWN)], agc_r.at[distance, way])

    def ahead(i):
        if i == 0:
            arrive(1, 0)
            arrive(1, 1)
            arrive_over(0)
            cross_wait(0, 0)
        elif i < 7:
            distance, way = (i + 1) // 2, (i + 1) % 2
            if way == 0:
                arrive(distance, 2)
                arrive(distance + 1, 0)
                arrive_over(distance)
                arrive(distance + 1, 1)
            cross_wait(distance, way)
        else:
            arrive(4, 2)
            arrive_over(4)
            cross_wait(4, 0)

    def backward_chunk(i, _):
        for at in range(RING - 1):
            pl.when(i == at)(functools.partial(ahead, at))
        away = (i + 1) // 2
        there = (z + jnp.where(i % 2 == 1, RING - away, away)) % RING
        span = rows_at(there * CHUNK, CHUNK)
        acc[...] += lax.dot_general(
            adj[span, :], grads[span, :], turn, preferred_element_type=F32
        )
        pl.when(i == 2)(w_stage2)
        pl.when(i == 4)(w_stage3)
        pl.when(i == 6)(w_stage4)
        return 0

    lax.fori_loop(0, RING - 1, backward_chunk, 0)

    def col_copy(i):
        mine = cols_b.at[rows_at(((r + i) % ROWS) * OWN, OWN)]
        return remote(mine, cols_in.at[i - 1], sent, col_r, row_dev(i))

    ahead(RING - 1)
    last_span = rows_at(((z + 4) % RING) * CHUNK, CHUNK)

    def last_part(k, _):
        pair = (r // 2 + 1 + k) % 4
        nodes = pl.ds(pl.multiple_of(pair * 2 * OWN, 2 * OWN), 2 * OWN)
        part_sum = acc[nodes, :] + lax.dot_general(
            adj[last_span, nodes], grads[last_span, :], turn, preferred_element_type=F32
        )
        acc[nodes, :] = part_sum
        cols_b[nodes, :] = part_sum.astype(BF16)
        for j in range(2):
            i = (2 * pair + j + ROWS - r) % ROWS

            def send(i=i):
                col_copy(i).start()

            pl.when(i > 0)(send)
        return 0

    lax.fori_loop(0, 4, last_part, 0)

    w_stage5()

    arrived_all(w_full.at[pl.ds(0, FEAT - PIECE)], w_r.at[4])
    src_again = column(src_deg)
    arrived_all(cols_in, col_r)
    total = acc[own_rows, :]
    for i in range(ROWS - 1):
        total = total + cols_in[i].astype(F32)
    hidden_out[...] = (src_again * total).astype(BF16)

    blocks = 2 * 14 + 2 * 32 + 18 + 2 * 21
    arrived_all(adj.at[pl.ds(0, blocks * OWN * HALF // COL_SPAN)], sent)
    w_rows_sent = 14 * PIECE // 2 + 13 * QUARTER
    arrived_all(part.at[0, pl.ds(0, w_rows_sent)], w_sent)


def finish(act, hidden, weight, w_sum, act_out, gf_out, gw_out):
    act_out[...] = act[...]
    gf_out[...] = lax.dot_general(
        hidden[...], weight[...], (((1,), (1,)), ((), ())), preferred_element_type=F32
    ).astype(BF16)
    full = w_sum[...].astype(F32)
    root = jnp.sqrt(jnp.sum(full * full) * (1.0 / (FEAT * FEAT)))
    gw_out[...] = full * jnp.minimum(1.0, 1.0 / (root + 1e-6))


def per_device(
    features, weight, src_degree, dst_degree, cotangent, tile_rows, tile_cols, tile_count, pattern
):
    vmem = pl.BlockSpec(memory_space=pltpu.VMEM)
    smem = pl.BlockSpec(memory_space=pltpu.SMEM)
    hbm = pl.BlockSpec(memory_space=pl.ANY)
    dma = pltpu.SemaphoreType.DMA
    block = (OWN, FEAT)
    scratch = [
        pltpu.VMEM((FEAT, FEAT), BF16),
        pltpu.VMEM(block, BF16),
        pltpu.VMEM((SLOTS, TILE // 8, TILE), jnp.int32),
        pltpu.VMEM((TABLE_ROWS, TILE), jnp.int32),
        pltpu.SMEM((TABLE_ROWS, TILE), jnp.int32),
        pltpu.VMEM((HALF, 2 * HALF), F32),
        pltpu.VMEM((COL_SPAN, FEAT), BF16),
        pltpu.VMEM((SLOTS + 1, TILE, TILE), BF16),
        pltpu.VMEM((ROW_SPAN, COL_SPAN), BF16),
        pltpu.VMEM((RING, CHUNK, FEAT), F32),
        pltpu.VMEM((RING, 2) + block, BF16),
        pltpu.VMEM((RING, 2) + block, BF16),
        pltpu.VMEM((RING, OWN, HALF), BF16),
        pltpu.VMEM((RING, OWN, HALF), BF16),
        pltpu.VMEM((2, 4, UNITS, OWN, HALF), BF16),
        pltpu.VMEM((2, 4, UNITS, OWN, HALF), BF16),
        pltpu.VMEM((OWN, HALF), BF16),
        pltpu.VMEM((OWN, HALF), BF16),
        pltpu.VMEM(block, F32),
        pltpu.VMEM((ROW_SPAN, FEAT), BF16),
        pltpu.VMEM((COL_SPAN, FEAT), F32),
        pltpu.VMEM((COL_SPAN, FEAT), BF16),
        pltpu.VMEM((ROWS - 1,) + block, BF16),
        pltpu.VMEM((FEAT, FEAT), F32),
        pltpu.VMEM((FEAT, FEAT), BF16),
        pltpu.VMEM((ROWS - 1, PIECE, FEAT), BF16),
        pltpu.VMEM((PIECE, FEAT), F32),
        pltpu.VMEM((3, QUARTER, FEAT), F32),
        pltpu.VMEM((RING, QUARTER, FEAT), F32),
        dma((4,)),
    ]
    scratch += [
        dma,
        dma,
        dma,
        dma((RING,)),
        dma((RING,)),
        dma((2, 4, UNITS)),
        dma,
        dma((2, 4, UNITS)),
        dma((5, 2)),
        dma((2, 6)),
        dma,
        dma((5,)),
    ]
    act, hidden, w_sum = pl.pallas_call(
        kernel,
        out_shape=(
            jax.ShapeDtypeStruct(block, BF16),
            jax.ShapeDtypeStruct(block, BF16),
            jax.ShapeDtypeStruct((FEAT, FEAT), BF16),
        ),
        in_specs=[vmem, hbm, vmem, vmem, hbm, vmem, vmem, smem, hbm],
        out_specs=(vmem, vmem, vmem),
        scratch_shapes=scratch,
        compiler_params=pltpu.CompilerParams(
            collective_id=0, has_side_effects=True, vmem_limit_bytes=60 * 1024 * 1024
        ),
        cost_estimate=pl.CostEstimate(
            flops=4 * ROW_SPAN * COL_SPAN * FEAT, bytes_accessed=3 << 20, transcendentals=0
        ),
    )(
        features,
        weight,
        src_degree.reshape(1, OWN),
        dst_degree.reshape(1, OWN),
        cotangent,
        tile_rows.reshape(1, OWN),
        tile_cols.reshape(1, OWN),
        tile_count,
        pattern,
    )
    return pl.pallas_call(
        finish,
        out_shape=(
            jax.ShapeDtypeStruct(block, BF16),
            jax.ShapeDtypeStruct(block, BF16),
            jax.ShapeDtypeStruct((FEAT, FEAT), F32),
        ),
        in_specs=[vmem] * 4,
        out_specs=(vmem, vmem, vmem),
    )(act, hidden, weight, w_sum)


def solution(mesh):
    placed = (
        P(("col", "row"), None),
        P(),
        P(("col", "row")),
        P(("row", "col")),
        P(("row", "col"), None),
        P(("row", "col")),
        P(("row", "col")),
        P(("row", "col")),
        P(("row", "col"), None, None),
    )
    return jax.shard_map(
        per_device,
        mesh=mesh,
        in_specs=placed,
        out_specs=(P(("row", "col"), None), P(("col", "row"), None), P()),
        check_vma=False,
    )
```

```python
import functools

import jax
import jax.numpy as jnp
from jax import lax
from jax.experimental import pallas as pl
from jax.experimental.pallas import tpu as pltpu
from jax.sharding import PartitionSpec as P

MESH = pl.DeviceIdType.MESH
F32 = jnp.float32
BF16 = jnp.bfloat16

FEAT = 256
HALF = 128
TILE = 128
SLOTS = 192
OWN = 192
ROWS = 8
RING = 8
TROWS = 48
TCOLS = 12
PLACES = TROWS * TCOLS
CHUNK = 4 * OWN
ROW_SPAN = RING * CHUNK
COL_SPAN = ROWS * OWN
PIECE = FEAT // ROWS
QUARTER = PIECE // 4
UNITS = 3
SUB = OWN // 2
TABLE_ROWS = 8
UNROLL = 4


RING_PLAN = (
    (1, ((0, 0, 0), (0, 1, 1))),
    (2, ((1, 1, 0),)),
    (3, ((1, 0, 1),)),
    (4, ((1, 0, 0), (1, 1, 1), (0, 2, 0), (0, 2, 1))),
    (5, ((2, 1, 0), (2, 0, 1))),
    (6, ((2, 0, 0), (2, 1, 1), (1, 2, 0), (1, 2, 1))),
    (7, ((3, 1, 0), (3, 0, 1))),
)


def remote(src, dst, send_sem, recv_sem, device):
    return pltpu.make_async_remote_copy(
        src_ref=src,
        dst_ref=dst,
        send_sem=send_sem,
        recv_sem=recv_sem,
        device_id=device,
        device_id_type=MESH,
    )


def rows_at(start, size):
    return pl.ds(pl.multiple_of(start, 8 if size < 16 else 32), size)


def kernel(
    feat,
    weight_hbm,
    src_deg,
    dst_deg,
    cot_hbm,
    tile_rows,
    tile_cols,
    tile_count,
    pattern_hbm,
    act_out,
    hidden_out,
    w_full,
    weight,
    cot,
    pattern,
    table_vec,
    table,
    deg_buf,
    s_all,
    tiles,
    adj,
    part,
    core_out,
    core_in,
    x_out,
    x_in,
    ring_out,
    ring_in,
    xhi_out,
    xhi_in,
    sums_buf,
    grads,
    acc,
    cols_b,
    cols_in,
    w_part,
    w_out,
    w_rows,
    w_piece,
    w_quart,
    w_ring,
    act_buf,
    load_sem,
    sent,
    w_sent,
    gat_r,
    core_r,
    x_r,
    ring_r,
    xhi_r,
    agr_r,
    agc_r,
    agx_r,
    col_r,
    w_r,
):
    r = lax.axis_index("row")
    c = lax.axis_index("col")
    z = c // 4
    quad = c % 4
    xhi = quad // 2
    core = quad % 2
    other_core = 1 - core
    other_xhi = 1 - xhi

    def row_dev(i):
        return {"row": (r + i) % ROWS}

    def quad_dev(i):
        return {"col": z * 4 + (quad + i) % 4}

    def z_dev(i):
        return {"col": ((z + i) % RING) * 4 + quad}

    core_dev = {"col": z * 4 + xhi * 2 + other_core}
    xhi_dev = {"col": z * 4 + other_xhi * 2 + core}
    ring_dev = [z_dev(1), z_dev(RING - 1)]

    loads = [
        pltpu.make_async_copy(pattern_hbm, pattern, load_sem.at[0]),
        pltpu.make_async_copy(weight_hbm, weight, load_sem.at[1]),
        pltpu.make_async_copy(cot_hbm, cot, load_sem.at[2]),
    ]
    for load in loads:
        load.start()

    barrier = pltpu.get_barrier_semaphore()

    def greet(device):
        pl.semaphore_signal(barrier, inc=1, device_id=device, device_id_type=MESH)

    def greet_rows(i, _):
        greet(row_dev(i))
        return 0

    lax.fori_loop(1, ROWS, greet_rows, 0)
    for device in (core_dev, xhi_dev, *ring_dev):
        greet(device)
    def upright(lane_values):
        deg_buf[:, 0:OWN] = jnp.broadcast_to(lane_values, (HALF, OWN))
        return deg_buf[...].T[0:OWN, :]

    def column(deg):
        turned = upright(lax.rsqrt(deg[...].astype(F32)))
        return jnp.concatenate([turned, turned], axis=1)

    deg_buf[...] = jnp.ones_like(deg_buf)

    src_scale = column(src_deg)
    own_rows = rows_at(r * OWN, OWN)
    s_all[own_rows, :] = (feat[...].astype(F32) * src_scale).astype(BF16)

    lane = lax.broadcasted_iota(jnp.int32, (1, OWN), 1)
    place = jnp.where(lane < tile_count[0], tile_rows[...] * TCOLS + tile_cols[...], -1)
    place_down = upright(place.astype(F32)).astype(jnp.int32)
    slot_down = lax.broadcasted_iota(jnp.int32, (SLOTS, TILE), 0)
    lanes = lax.broadcasted_iota(jnp.int32, (SLOTS, TILE), 1)

    def last_slot(named):
        last = jnp.max(jnp.where(named, slot_down, -1), axis=0, keepdims=True)
        return jnp.where(last < 0, SLOTS, last)

    for row in range(TROWS // 8):
        asked = (row * 8 + lanes // 16) * TCOLS + lanes % 16
        named = (place_down == asked) & (lanes % 16 < TCOLS)
        table_vec[row : row + 1, :] = last_slot(named)
    for row, start, size in ((6, 0, TILE), (7, TILE, SLOTS - TILE)):
        asked = place[:, start : start + size]
        if size < TILE:
            asked = jnp.concatenate([asked, jnp.full((1, TILE - size), -2, jnp.int32)], axis=1)
        named = (place_down == asked) & (slot_down < lanes + start) & (place_down >= 0)
        table_vec[row : row + 1, :] = last_slot(named)
    to_smem = pltpu.make_async_copy(table_vec, table, load_sem.at[3])
    to_smem.start()

    pl.semaphore_wait(barrier, ROWS - 1 + 4)

    def gather_copy(i, sender):
        span = rows_at(sender * OWN, OWN)
        return remote(s_all.at[span], s_all.at[span], sent, gat_r, row_dev(i))

    def gather_start(i, _):
        gather_copy(i, r).start()
        return 0

    lax.fori_loop(1, ROWS, gather_start, 0)

    to_smem.wait()
    loads[0].wait()

    tiles[SLOTS] = jnp.zeros((TILE, TILE), BF16)
    bit = lax.broadcasted_iota(jnp.int32, (TILE // 8, 8, TILE), 1)

    def unpack(row, first):
        def one(k, _):
            words = jnp.broadcast_to(pattern[first + k][:, None, :], (TILE // 8, 8, TILE))
            bits = jnp.bitwise_and(jnp.right_shift(words, bit), 1).reshape(TILE, TILE)
            tiles[first + k] = bits.astype(F32).astype(BF16) + tiles[table[row, k]]
            return 0

        return one

    lax.fori_loop(0, TILE, unpack(6, 0), 0, unroll=UNROLL)
    lax.fori_loop(0, SLOTS - TILE, unpack(7, TILE), 0, unroll=UNROLL)

    def assemble(row, _):
        for t in range(8):
            for j in range(TCOLS):
                adj[rows_at((row * 8 + t) * TILE, TILE), j * TILE : (j + 1) * TILE] = tiles[
                    table[row, t * 16 + j]
                ]
        return 0

    lax.fori_loop(0, TROWS // 8, assemble, 0)

    def arrived_all(ref, sem):
        pltpu.make_async_copy(ref, ref, sem).wait()

    arrived_all(s_all.at[pl.ds(0, COL_SPAN - OWN)], gat_r)

    def core_copy(i):
        return remote(core_out.at[i], core_in.at[i], sent, core_r.at[i], core_dev)

    LOW, HIGH = slice(0, HALF), slice(HALF, FEAT)

    def core_sum(i, xh, lanes):
        mine = part[i, rows_at((2 * xh + core) * OWN, OWN), lanes]
        return mine + core_in[i, xh, :, lanes].astype(F32)

    def x_copy(i):
        return remote(x_out.at[i], x_in.at[i], sent, x_r.at[i], xhi_dev)

    def x_wait(i):
        x_copy(i).wait_recv()

    def merge(i):
        core_copy(i).wait_recv()
        x_out[i] = core_sum(i, other_xhi, HIGH).astype(BF16)
        x_copy(i).start()

    def unit_sum(i, unit):
        if unit < 2:
            return core_sum(i, (other_xhi, xhi)[unit], LOW)
        return core_sum(i, xhi, HIGH) + x_in[i].astype(F32)

    def ring_rows(way, step, unit):
        if step > 0:
            return slice(0, OWN)
        if unit < 2:
            return slice(0, OWN) if unit == way else None
        return slice(way * SUB, (way + 1) * SUB)

    def ring_copy(way, step, unit):
        rows = ring_rows(way, step, unit)
        rows = pl.ds(rows.start, rows.stop - rows.start)
        return remote(
            ring_out.at[way, step, unit, rows],
            ring_in.at[way, step, unit, rows],
            sent,
            ring_r.at[way, step, unit],
            ring_dev[way],
        )

    def ring_step(step, unit, way):
        rows = ring_rows(way, step, unit)
        if step == 0:
            ring_out[way, 0, unit, rows, :] = unit_sum(0, unit)[rows].astype(BF16)
            ring_copy(way, 0, unit).start()
            return
        total = unit_sum(2 * step - 1 + way, unit)
        arrived = ring_rows(way, step - 1, unit)
        if arrived is None:
            ring_out[way, step, unit] = total.astype(BF16)
        else:
            ring_copy(way, step - 1, unit).wait_recv()
            for half in (slice(0, SUB), slice(SUB, OWN)):
                block = total[half]
                if arrived.start <= half.start and half.stop <= arrived.stop:
                    block = block + ring_in[way, step - 1, unit, half, :].astype(F32)
                ring_out[way, step, unit, half, :] = block.astype(BF16)
        ring_copy(way, step, unit).start()

    def home_sum(unit):
        total = unit_sum(7, unit)
        for way in range(2):
            ring_copy(way, 3, unit).wait_recv()
            total = total + ring_in[way, 3, unit].astype(F32)
        return total

    def forward_chunk(i, _):
        back = 4 - (i + 1) // 2
        there = (z + jnp.where(i % 2 == 1, back, RING - back)) % RING
        part[i] = jnp.dot(
            adj[rows_at(there * CHUNK, CHUNK), :], s_all[...], preferred_element_type=F32
        )
        for xh in range(2):
            theirs = part[i, rows_at((2 * xh + other_core) * OWN, OWN), :]
            core_out[i, xh] = theirs.astype(BF16)
        core_copy(i).start()
        pl.when(i > 0)(functools.partial(merge, i - 1))
        for at, steps in RING_PLAN:
            for step, unit, way in steps:
                if unit == 2 and (step > 0 or way == 0):
                    slot = 2 * step - 1 + way if step else 0
                    pl.when(i == at)(functools.partial(x_wait, slot))
                pl.when(i == at)(functools.partial(ring_step, step, unit, way))
        return 0

    lax.fori_loop(0, RING, forward_chunk, 0)

    merge(7)
    ring_step(3, 0, 0)
    ring_step(3, 1, 1)
    for way in range(2):
        x_copy(3 + way).wait_recv()
        ring_step(2, 2, way)
    xhi_out[...] = home_sum(0).astype(BF16)
    xhi_copy = remote(xhi_out, xhi_in, sent, xhi_r, xhi_dev)
    xhi_copy.start()
    for way in range(2):
        x_copy(5 + way).wait_recv()
        ring_step(3, 2, way)
    x_copy(7).wait_recv()
    sums_buf[:, LOW] = home_sum(1)
    loads[1].wait()
    loads[2].wait()
    dst_scale = column(dst_deg)
    sums_buf[:, HIGH] = home_sum(2)
    xhi_copy.wait_recv()
    sums_buf[:, LOW] += xhi_in[...].astype(F32)
    sums = sums_buf[...]

    high = sums.astype(BF16)
    low = (sums - high.astype(F32)).astype(BF16)

    def preact_of(lanes):
        mixed = jnp.dot(high, weight[:, lanes], preferred_element_type=F32)
        mixed = mixed + jnp.dot(low, weight[:, lanes], preferred_element_type=F32)
        return dst_scale[:, lanes] * mixed

    def decay_of(preact):
        return jnp.exp(jnp.minimum(preact, 0.0))

    grad_rows = rows_at(z * CHUNK + quad * OWN, OWN)

    def put_grads(lanes):
        preact = preact_of(lanes)
        decay = decay_of(preact)
        slope = jnp.where(preact > 0, 1.0, decay)
        grads[grad_rows, lanes] = (
            dst_scale[:, lanes] * (cot[:, lanes].astype(F32) * slope)
        ).astype(BF16)
        act_buf[:, lanes] = jnp.where(preact > 0, preact, decay - 1.0).astype(BF16)


    def origin(way, distance):
        return (z + (RING - distance if way == 0 else distance)) % RING

    def block(chip, distance, way, unit, cr):
        xh = xhi if unit < 2 else other_xhi
        start, size = 0, OWN
        if distance == 4 and unit in (0, 3):
            start, size = way * SUB, SUB
        rows = rows_at(chip * CHUNK + (2 * xh + cr) * OWN + start, size)
        return grads.at[rows, pl.ds(0 if unit in (1, 2) else HALF, HALF)]

    def ways(distance, unit):
        if distance == 0:
            return (0,)
        if distance == 4 and unit in (1, 2):
            return (unit - 1,)
        return (0, 1)

    def around(way, distance, unit, chip):
        ref = block(chip, distance, way, unit, core)
        return remote(ref, ref, sent, agr_r.at[way, distance - 1, unit], ring_dev[way])

    def across(way, distance, unit, cr):
        ref = block(origin(way, distance), distance, way, unit, cr)
        return remote(ref, ref, sent, agc_r.at[distance, 0 if distance == 4 else way], core_dev)

    def over(way, distance, unit):
        at = distance if unit in (0, 3) else 5
        ref = block(origin(way, distance), distance, way, unit, core)
        return remote(ref, ref, sent, agx_r.at[way, at], xhi_dev)

    put_grads(LOW)
    over(0, 0, 1).start()
    put_grads(HIGH)
    act_copy = pltpu.make_async_copy(act_buf, act_out, load_sem.at[0])
    act_copy.start()
    for way in range(2):
        around(way, 1, 0, z).start()
    over(0, 0, 0).start()
    for unit in range(2):
        across(0, 0, unit, core).start()

    turn = (((0,), (0,)), ((), ()))
    grad_own = grads[grad_rows, :]
    w_part[...] = lax.dot_general(high, grad_own, turn, preferred_element_type=F32)
    w_part[...] += lax.dot_general(low, grad_own, turn, preferred_element_type=F32)
    w_out[...] = w_part[...].astype(BF16)

    def w1_copy(i):
        mine = w_out.at[rows_at(((r + i) % ROWS) * PIECE, PIECE)]
        return remote(mine, w_rows.at[i - 1], w_sent, w_r.at[0], row_dev(i))

    def w2_copy(i):
        start = r * PIECE + ((quad + i) % 4) * QUARTER
        mine = w_part.at[rows_at(start, QUARTER)]
        return remote(mine, w_quart.at[i - 1], w_sent, w_r.at[1], quad_dev(i))

    def w3_copy(i, sender):
        return remote(
            w_ring.at[sender], w_ring.at[sender], w_sent, w_r.at[2], z_dev(i)
        )

    def w4_copy(i, sender):
        ref = w_piece.at[rows_at(sender * QUARTER, QUARTER)]
        return remote(ref, ref, w_sent, w_r.at[3], quad_dev(i))

    def w5_copy(i, sender):
        ref = w_full.at[rows_at(sender * PIECE, PIECE)]
        return remote(ref, ref, w_sent, w_r.at[4], row_dev(i))

    def each(count, action):
        def body(i, _):
            action(i)
            return 0

        lax.fori_loop(1, count, body, 0)

    def w_stage1():
        each(ROWS, lambda i: w1_copy(i).start())

    def w_stage2():
        arrived_all(w_rows, w_r.at[0])
        piece = rows_at(r * PIECE, PIECE)
        total = w_part[piece, :]
        for i in range(ROWS - 1):
            total = total + w_rows[i].astype(F32)
        w_part[piece, :] = total
        each(4, lambda i: w2_copy(i).start())

    def w_stage3():
        arrived_all(w_quart, w_r.at[1])
        total = w_part[rows_at(r * PIECE + quad * QUARTER, QUARTER), :]
        for i in range(3):
            total = total + w_quart[i]
        w_ring[z] = total
        each(RING, lambda i: w3_copy(i, z).start())

    def w_stage4():
        arrived_all(w_ring.at[pl.ds(0, RING - 1)], w_r.at[2])
        total = w_ring[0]
        for i in range(1, RING):
            total = total + w_ring[i]
        w_piece[rows_at(quad * QUARTER, QUARTER), :] = total
        each(4, lambda i: w4_copy(i, quad).start())

    def w_stage5():
        arrived_all(w_piece.at[pl.ds(0, 3 * QUARTER)], w_r.at[3])
        w_full[rows_at(r * PIECE, PIECE), :] = w_piece[...].astype(BF16)
        each(ROWS, lambda i: w5_copy(i, r).start())

    w_stage1()

    for way in range(2):
        around(way, 1, 1, z).start()
    over(0, 0, 2).wait_recv()
    for way in range(2):
        around(way, 1, 2, z).start()
    across(0, 0, 2, core).start()

    acc[...] = jnp.zeros_like(acc)

    def arrive(distance, unit):
        for way in ways(distance, unit):
            chip = origin(way, distance)
            around(way, distance, unit, chip).wait_recv()
            if distance < 4 and way in ways(distance + 1, unit):
                around(way, distance + 1, unit, chip).start()
            across(way, distance, unit, core).start()
            if unit == 0:
                over(way, distance, 0).start()

    def arrive_over(distance):
        for way in ways(distance, 3):
            over(way, distance, 3).wait_recv()
            across(way, distance, 3, core).start()

    def cross_wait(distance, way):
        arrived_all(grads.at[pl.ds(0, 2 * OWN)], agc_r.at[distance, way])

    def ahead(i):
        if i == 0:
            arrive(1, 0)
            arrive(1, 1)
            arrive_over(0)
            cross_wait(0, 0)
        elif i < 7:
            distance, way = (i + 1) // 2, (i + 1) % 2
            if way == 0:
                arrive(distance, 2)
                arrive(distance + 1, 0)
                arrive_over(distance)
                arrive(distance + 1, 1)
            cross_wait(distance, way)
        else:
            arrive(4, 2)
            arrive_over(4)
            cross_wait(4, 0)

    def backward_chunk(i, _):
        for at in range(RING - 1):
            pl.when(i == at)(functools.partial(ahead, at))
        away = (i + 1) // 2
        there = (z + jnp.where(i % 2 == 1, RING - away, away)) % RING
        span = rows_at(there * CHUNK, CHUNK)
        acc[...] += lax.dot_general(
            adj[span, :], grads[span, :], turn, preferred_element_type=F32
        )
        pl.when(i == 2)(w_stage2)
        pl.when(i == 4)(w_stage3)
        pl.when(i == 6)(w_stage4)
        return 0

    lax.fori_loop(0, RING - 1, backward_chunk, 0)

    def col_copy(i):
        mine = cols_b.at[rows_at(((r + i) % ROWS) * OWN, OWN)]
        return remote(mine, cols_in.at[i - 1], sent, col_r, row_dev(i))

    ahead(RING - 1)
    last_span = rows_at(((z + 4) % RING) * CHUNK, CHUNK)

    def last_part(k, _):
        pair = (r // 2 + 2 + k * (k + 1) // 2 * 3) % 4
        nodes = pl.ds(pl.multiple_of(pair * 2 * OWN, 2 * OWN), 2 * OWN)
        part_sum = acc[nodes, :] + lax.dot_general(
            adj[last_span, nodes], grads[last_span, :], turn, preferred_element_type=F32
        )
        acc[nodes, :] = part_sum
        cols_b[nodes, :] = part_sum.astype(BF16)
        for j in range(2):
            i = (2 * pair + j + ROWS - r) % ROWS

            def send(i=i):
                col_copy(i).start()

            pl.when(i > 0)(send)
        return 0

    lax.fori_loop(0, 4, last_part, 0)

    w_stage5()

    arrived_all(w_full.at[pl.ds(0, FEAT - PIECE)], w_r.at[4])
    src_again = column(src_deg)
    arrived_all(cols_in, col_r)
    total = acc[own_rows, :]
    for i in range(ROWS - 1):
        total = total + cols_in[i].astype(F32)
    hidden_out[...] = (src_again * total).astype(BF16)

    act_copy.wait()

    blocks = 2 * 14 + 2 * 32 + 18 + 2 * 21
    arrived_all(adj.at[pl.ds(0, blocks * OWN * HALF // COL_SPAN)], sent)
    w_rows_sent = 14 * PIECE // 2 + 13 * QUARTER
    arrived_all(part.at[0, pl.ds(0, w_rows_sent)], w_sent)


def finish(act, hidden, weight, w_sum, act_out, gf_out, gw_out):
    act_out[...] = act[...]
    gf_out[...] = lax.dot_general(
        hidden[...], weight[...], (((1,), (1,)), ((), ())), preferred_element_type=F32
    ).astype(BF16)
    full = w_sum[...].astype(F32)
    root = jnp.sqrt(jnp.sum(full * full) * (1.0 / (FEAT * FEAT)))
    gw_out[...] = full * jnp.minimum(1.0, 1.0 / (root + 1e-6))


def per_device(
    features, weight, src_degree, dst_degree, cotangent, tile_rows, tile_cols, tile_count, pattern
):
    vmem = pl.BlockSpec(memory_space=pltpu.VMEM)
    smem = pl.BlockSpec(memory_space=pltpu.SMEM)
    hbm = pl.BlockSpec(memory_space=pl.ANY)
    dma = pltpu.SemaphoreType.DMA
    block = (OWN, FEAT)
    scratch = [
        pltpu.VMEM((FEAT, FEAT), BF16),
        pltpu.VMEM(block, BF16),
        pltpu.VMEM((SLOTS, TILE // 8, TILE), jnp.int32),
        pltpu.VMEM((TABLE_ROWS, TILE), jnp.int32),
        pltpu.SMEM((TABLE_ROWS, TILE), jnp.int32),
        pltpu.VMEM((HALF, 2 * HALF), F32),
        pltpu.VMEM((COL_SPAN, FEAT), BF16),
        pltpu.VMEM((SLOTS + 1, TILE, TILE), BF16),
        pltpu.VMEM((ROW_SPAN, COL_SPAN), BF16),
        pltpu.VMEM((RING, CHUNK, FEAT), F32),
        pltpu.VMEM((RING, 2) + block, BF16),
        pltpu.VMEM((RING, 2) + block, BF16),
        pltpu.VMEM((RING, OWN, HALF), BF16),
        pltpu.VMEM((RING, OWN, HALF), BF16),
        pltpu.VMEM((2, 4, UNITS, OWN, HALF), BF16),
        pltpu.VMEM((2, 4, UNITS, OWN, HALF), BF16),
        pltpu.VMEM((OWN, HALF), BF16),
        pltpu.VMEM((OWN, HALF), BF16),
        pltpu.VMEM(block, F32),
        pltpu.VMEM((ROW_SPAN, FEAT), BF16),
        pltpu.VMEM((COL_SPAN, FEAT), F32),
        pltpu.VMEM((COL_SPAN, FEAT), BF16),
        pltpu.VMEM((ROWS - 1,) + block, BF16),
        pltpu.VMEM((FEAT, FEAT), F32),
        pltpu.VMEM((FEAT, FEAT), BF16),
        pltpu.VMEM((ROWS - 1, PIECE, FEAT), BF16),
        pltpu.VMEM((PIECE, FEAT), F32),
        pltpu.VMEM((3, QUARTER, FEAT), F32),
        pltpu.VMEM((RING, QUARTER, FEAT), F32),
        pltpu.VMEM(block, BF16),
        dma((4,)),
    ]
    scratch += [
        dma,
        dma,
        dma,
        dma((RING,)),
        dma((RING,)),
        dma((2, 4, UNITS)),
        dma,
        dma((2, 4, UNITS)),
        dma((5, 2)),
        dma((2, 6)),
        dma,
        dma((5,)),
    ]
    act, hidden, w_sum = pl.pallas_call(
        kernel,
        out_shape=(
            jax.ShapeDtypeStruct(block, BF16),
            jax.ShapeDtypeStruct(block, BF16),
            jax.ShapeDtypeStruct((FEAT, FEAT), BF16),
        ),
        in_specs=[vmem, hbm, vmem, vmem, hbm, vmem, vmem, smem, hbm],
        out_specs=(hbm, vmem, vmem),
        scratch_shapes=scratch,
        compiler_params=pltpu.CompilerParams(
            collective_id=0, has_side_effects=True, vmem_limit_bytes=60 * 1024 * 1024
        ),
        cost_estimate=pl.CostEstimate(
            flops=4 * ROW_SPAN * COL_SPAN * FEAT, bytes_accessed=3 << 20, transcendentals=0
        ),
    )(
        features,
        weight,
        src_degree.reshape(1, OWN),
        dst_degree.reshape(1, OWN),
        cotangent,
        tile_rows.reshape(1, OWN),
        tile_cols.reshape(1, OWN),
        tile_count,
        pattern,
    )
    return pl.pallas_call(
        finish,
        out_shape=(
            jax.ShapeDtypeStruct(block, BF16),
            jax.ShapeDtypeStruct(block, BF16),
            jax.ShapeDtypeStruct((FEAT, FEAT), F32),
        ),
        in_specs=[vmem] * 4,
        out_specs=(vmem, vmem, vmem),
    )(act, hidden, weight, w_sum)


def solution(mesh):
    placed = (
        P(("col", "row"), None),
        P(),
        P(("col", "row")),
        P(("row", "col")),
        P(("row", "col"), None),
        P(("row", "col")),
        P(("row", "col")),
        P(("row", "col")),
        P(("row", "col"), None, None),
    )
    return jax.shard_map(
        per_device,
        mesh=mesh,
        in_specs=placed,
        out_specs=(P(("row", "col"), None), P(("col", "row"), None), P()),
        check_vma=False,
    )
```
